128 devices in a mesh: prow: 16 (over x, z), pcol: 8 (over y, core).
Axes of the slice: x: 4, y: 4, z: 4, core: 2. Of those that a mesh axis runs over, the one named last changes fastest.
Arguments:
- matrix: float32 [20480, 20480], P('prow', 'pcol'), may hold values from -56 to 56
Outputs:
- reduced: float32 [20480, 20480], P('prow', 'pcol')
The draws below stay inside these ranges and needn't reach their ends.
All inputs are finite; a program needn't handle non-finite values.
Results may differ from the reference program's by a relative error of at most 0.000096.
Values sent between devices are 32-bit elements; how exact they have to be, the bound alone decides.
No kernel may reach another device: no remote copies, remote signals or barrier semaphores. Data moves between devices by JAX's collectives and lax.ppermute only.
A program may use at most 128 MiB of HBM per device.

```python
import jax
import jax.numpy as jnp
from jax import lax

PANEL = 128
ORDER = 20480


def draw_matrix(key, part):
    row_ids = jnp.arange(ORDER)
    base = jnp.clip(jax.random.normal(key, (ORDER, ORDER), jnp.float32), -6.0, 6.0)
    upper = row_ids[:, None] <= row_ids[None, :]
    sym = jnp.where(upper, base, base.T)
    spread = jax.random.uniform(jax.random.fold_in(key, 11), (ORDER,), jnp.float32)
    scales = jnp.exp(jnp.log(3.2) * spread) * jnp.sqrt(1.0 + 2.0 * row_ids.astype(jnp.float32) / ORDER)
    top_rows = (row_ids >= PANEL) & (row_ids < 2 * PANEL)
    first = row_ids < PANEL
    damp = jnp.where(top_rows[:, None] & first[None, :] | first[:, None] & top_rows[None, :], 0.25, 1.0)
    return 0.3 * sym * scales[:, None] * scales[None, :] * damp


def setup_inputs(seed: int = 0) -> dict:
    key_list = jax.random.split(jax.random.key(seed), 2)
    matrix = draw_matrix(jax.random.fold_in(key_list[1], 71), 0)
    return {"matrix": matrix}


def reference(matrix):
    high = lax.Precision.HIGHEST
    row_ids = jnp.arange(ORDER)
    panel = jnp.where(row_ids[:, None] >= PANEL, matrix[:, :PANEL], 0.0)
    gram = jnp.dot(panel.T, panel, precision=high)
    lower = jnp.linalg.cholesky(gram)
    basis = jax.scipy.linalg.solve_triangular(lower, panel.T, lower=True).T
    ident = (row_ids[:, None] - PANEL == jnp.arange(PANEL)[None, :]).astype(jnp.float32)
    vectors = basis - ident
    top_basis = basis[PANEL:2 * PANEL]
    shifted = jnp.eye(PANEL, dtype=jnp.float32) - top_basis.T
    factor = jnp.linalg.cholesky(jnp.dot(shifted.T, shifted, precision=high))
    coupling = jax.scipy.linalg.cho_solve((factor, True), shifted.T)
    image = jnp.dot(matrix, vectors, precision=high)
    inner = jnp.dot(vectors.T, image, precision=high)
    middle = jnp.dot(jnp.dot(coupling, inner, precision=high), coupling.T, precision=high)
    correction = jnp.dot(image, coupling.T, precision=high) - 0.5 * jnp.dot(vectors, middle, precision=high)
    left_side = jnp.concatenate([vectors, correction], axis=1)
    right_side = jnp.concatenate([correction, vectors], axis=1)
    return matrix - jnp.dot(left_side, right_side.T, precision=high)
```

```python
import jax
import jax.numpy as jnp
from jax import lax
from jax.experimental import pallas as pl
from jax.experimental.pallas import tpu as pltpu
from jax.sharding import PartitionSpec as P

W = 128
NR = 16
NC = 8
STEP = 256
WIDE = 512
F32 = jnp.float32
BF16 = jnp.bfloat16
SM = pl.BlockSpec(memory_space=pltpu.SMEM)
HB = pl.BlockSpec(memory_space=pltpu.HBM)


def shape(*dims, dtype=F32):
    return jax.ShapeDtypeStruct(dims, dtype)


def exact(a, b, ca, cb):
    return lax.dot_general(
        a, b, (((ca,), (cb,)), ((), ())), precision=lax.Precision.HIGHEST, preferred_element_type=F32
    )


def split(x):
    hi = x.astype(BF16)
    return hi, (x - hi.astype(F32)).astype(BF16)


def bdot(a, b, ca, cb):
    return lax.dot_general(a, b, (((ca,), (cb,)), ((), ())), preferred_element_type=F32)


def three(a, b, ca, cb):
    (ah, al), (bh, bl) = a, b
    return bdot(ah, bh, ca, cb) + (bdot(ah, bl, ca, cb) + bdot(al, bh, ca, cb))


def dot3(a, b, ca, cb):
    return three(split(a), split(b), ca, cb)


def iota2(dims, dim):
    return lax.broadcasted_iota(jnp.int32, dims, dim)


def run(copies):
    for copy in copies:
        copy.start()
    return copies


def wait(copies):
    for copy in copies:
        copy.wait()


def call(kernel, name, flops, args, outs, scratch, sems):
    single = not isinstance(outs, list)
    out_list = [outs] if single else outs
    size = sum(4 * a.size for a in args[1:]) + sum(4 * o.size for o in out_list)

    def body(*refs):
        n = len(args)
        m = n + len(out_list)
        sem = refs[-1]
        used = []

        def copy(src, dst):
            used.append(None)
            return pltpu.make_async_copy(src, dst, sem.at[len(used) - 1])

        kernel(refs[0], refs[1:n], refs[n:m], refs[m:-1], copy)

    result = pl.pallas_call(
        body,
        in_specs=[SM] + [HB] * (len(args) - 1),
        out_specs=[HB] * len(out_list),
        out_shape=out_list,
        scratch_shapes=[pltpu.VMEM(s.shape, s.dtype) for s in scratch] + [pltpu.SemaphoreType.DMA((sems,))],
        compiler_params=pltpu.CompilerParams(vmem_limit_bytes=60 * 1024 * 1024),
        cost_estimate=pl.CostEstimate(flops=int(flops), bytes_accessed=int(size), transcendentals=0),
        name=name,
    )(*args)
    return result[0] if single else result


def load_panel(rc, held, other, buf, copy):
    half = held.shape[0]
    at = pl.multiple_of(rc[2], half)
    return run([copy(held, buf.at[pl.ds(at, half)]), copy(other, buf.at[pl.ds(half - at, half)])])


def clear_top(rc, buf):
    @pl.when(rc[0] == 0)
    def _():
        buf[:W] = jnp.zeros((W, W), F32)


def gram_kernel(rc, ins, outs, bufs, copy):
    buf, out = bufs
    wait(load_panel(rc, ins[0], ins[1], buf, copy))
    clear_top(rc, buf)
    p = split(buf[...])
    g = three(p, p, 0, 0).reshape(NR, 8, W)
    t = jnp.where(rc[0] == 0, buf[W : 2 * W], 0.0).reshape(NR, 8, W)
    out[...] = jnp.concatenate([g, t], 1)
    wait(run([copy(out, outs[0])]))


def lane(x, k):
    return jnp.broadcast_to(x[:, k : k + 1], (8, W))


def row(x, k):
    return jnp.broadcast_to(x[k : k + 1], (8, W))


def eliminate(g, tiles_out):
    lanes = iota2((8, W), 1)
    subs = iota2((8, W), 0)
    tiles = [g[8 * t : 8 * t + 8] for t in range(W // 8)]
    for k in range(0, W, 2):
        t0, o = k // 8, k % 8
        top = tiles[t0]
        at0, at1 = lanes == k, lanes == k + 1
        both = at0 | at1
        c0, c1 = lane(top, k), lane(top, k + 1)
        a, b, d = row(c0, o), row(c1, o), row(c1, o + 1)
        r0 = jnp.where(at1, 0.0, jnp.where(at0, 1.0, row(top, o)))
        r1 = jnp.where(at0, 0.0, jnp.where(at1, 1.0, row(top, o + 1)))
        ia = 1.0 / a
        ba = b * ia
        n1 = r1 - ba * r0
        s = d - b * ba
        q1 = n1 * (1.0 / s)
        q0 = r0 * ia - ba * q1
        for t in range(t0, W // 8):
            m = tiles[t]
            if t > t0:
                tiles[t] = jnp.where(both, 0.0, m) - lane(m, k) * q0 - lane(m, k + 1) * q1
            elif o < 6:
                tiles[t] = jnp.where(subs > o + 1, jnp.where(both, 0.0, m) - c0 * q0 - c1 * q1, m)
        if o == 0:
            final = jnp.zeros((8, W), F32)
        final = jnp.where(subs == o, r0 * lax.rsqrt(a), jnp.where(subs == o + 1, n1 * lax.rsqrt(s), final))
        if o == 6:
            tiles_out.append(final)
        yield


def lower_part(tiles):
    i, j = iota2((W, W), 0), iota2((W, W), 1)
    return jnp.where(i >= j, jnp.concatenate(tiles, 0), 0.0)


def inverse_factor(g):
    tiles = []
    for _ in eliminate(g, tiles):
        pass
    return lower_part(tiles)


def first_kernel(rc, ins, outs, bufs, copy):
    a_ref, held, other, small = ins
    buf, panel, acc, rows_out, msg, linv = bufs
    rows, cols = buf.shape
    n = rows // STEP
    get = run([copy(small, msg)])
    first = load_panel(rc, held, other, panel, copy)
    copies = run([copy(a_ref.at[pl.ds(k * STEP, STEP)], buf.at[pl.ds(k * STEP, STEP)]) for k in range(n)])
    wait(get)
    gram = msg[:, :8].reshape(W, W)
    tiles = []
    steps = eliminate(gram, tiles)
    wait(first)
    clear_top(rc, panel)
    ph, plow = split(panel[...])
    both = jnp.concatenate([ph, plow], 1)
    blocks = cols // WIDE
    each = -(-W // (2 * n * blocks))
    for k in range(n):
        copies[k].wait()
        lo, up = k * STEP, (k + 1) * STEP
        for b in range(blocks):
            for _ in range(each):
                next(steps, None)
            sl = slice(b * WIDE, (b + 1) * WIDE)
            ah, al = split(buf[lo:up, sl])
            x = bdot(both[lo:up], ah, 0, 0)
            x = x[:W] + (x[W:] + bdot(ph[lo:up], al, 0, 0))
            if k == 0:
                acc[:, sl] = x
            else:
                acc[:, sl] += x
    for _ in steps:
        pass
    inverse = lower_part(tiles)
    linv[...] = inverse
    sent = run([copy(linv, outs[1])])

    @pl.when(rc[0] == 0)
    def _():
        ls = split(exact(gram, inverse, 1, 1))
        for b in range(blocks):
            sl = slice(b * WIDE, (b + 1) * WIDE)
            acc[:, sl] -= three(ls, split(buf[W : 2 * W, sl]), 1, 0)

    for b in range(blocks):
        sl = slice(b * WIDE, (b + 1) * WIDE)
        rows_out[sl] = acc[:, sl].T
    piece = outs[0].shape[1]
    wait(sent + run([copy(rows_out.at[pl.ds(k * piece, piece)], outs[0].at[k]) for k in range(NR)]))


def coupling_kernel(rc, ins, outs, bufs, copy):
    msg, linv, out = bufs
    wait(run([copy(ins[0], msg), copy(ins[1], linv)]))
    i, j = iota2((W, W), 0), iota2((W, W), 1)
    shifted = jnp.where(i == j, 1.0, 0.0) - exact(linv[...], msg[:, 8:].reshape(W, W), 1, 1)
    finv = inverse_factor(exact(shifted, shifted, 0, 0))
    out[...] = exact(finv, exact(finv, shifted, 1, 1), 0, 0)
    wait(run([copy(out, outs[0])]))


def piece_kernel(rc, ins, outs, bufs, copy):
    msg, linv, out = bufs
    wait(run([copy(ins[0], msg), copy(ins[1], linv)]))
    out[...] = dot3(jnp.sum(msg[...], 0), linv[...], 1, 1)
    wait(run([copy(out, outs[0].at[k]) for k in range(NR)] + [copy(out, outs[1])]))


def vectors_kernel(rc, ins, outs, bufs, copy):
    p, linv, v = bufs
    cols = p.shape[0]
    wait(run([copy(ins[0], p), copy(ins[1], linv)]))
    ls = split(linv[...])
    for b in range(cols // WIDE):
        sl = slice(b * WIDE, (b + 1) * WIDE)
        at = iota2((W, WIDE), 1) + (rc[1] * cols + b * WIDE - W)
        x = three(ls, split(p[sl]), 1, 1)
        x = jnp.where(at < 0, 0.0, x) - jnp.where(at == iota2((W, WIDE), 0), 1.0, 0.0)
        v[0, :, sl], v[1, :, sl] = split(x)
    wait(run([copy(v, outs[0])]))


def inner_kernel(rc, ins, outs, bufs, copy):
    v, y, out = bufs
    wait(run([copy(ins[0], v), copy(ins[1], y)]))
    out[...] = three((v[0], v[1]), split(y[...].reshape(v.shape[2], W)), 1, 0)
    wait(run([copy(out, outs[0].at[k]) for k in range(NC)]))


def sides_kernel(rc, ins, outs, bufs, copy):
    held, other, y_r, y_c, linv_ref, coup_ref = ins
    panel, yr, yc, linv, coup, left, wide = bufs
    rows, cols = panel.shape[0], wide.shape[1]
    small = run([copy(linv_ref, linv), copy(coup_ref, coup), copy(y_c, yc)])
    more = load_panel(rc, held, other, panel, copy) + run([copy(y_r, yr)])
    wait(small)
    ls, cs = split(linv[...]), split(coup[...])
    flat = yc.reshape(cols, W)
    for b in range(cols // WIDE):
        sl = slice(b * WIDE, (b + 1) * WIDE)
        wide[:, sl] = three(cs, split(flat[sl]), 1, 1)
    last = run([copy(wide, outs[1])])
    wait(more)
    clear_top(rc, panel)
    for k in range(rows // STEP):
        sl = slice(k * STEP, (k + 1) * STEP)
        ids = rc[0] * rows + k * STEP + iota2((STEP, W), 0)
        v = three(split(panel[sl]), ls, 1, 1) - jnp.where(ids - W == iota2((STEP, W), 1), 1.0, 0.0)
        left[0, sl, :W], left[1, sl, :W] = split(v)
        left[0, sl, W:], left[1, sl, W:] = split(three(split(yr[sl]), cs, 1, 1))
    wait(last + run([copy(left, outs[0])]))


def last_kernel(rc, ins, outs, bufs, copy):
    a_ref, s_ref, coup_ref, left_ref, wide_ref, v_ref = ins
    buf, s, coup, left, wide, right = bufs
    rows, cols = buf.shape
    n = rows // STEP
    small = run([copy(s_ref, s), copy(coup_ref, coup)])
    mid = run([copy(v_ref, right.at[:, pl.ds(W, W)]), copy(wide_ref, wide)])
    copies = run([copy(a_ref.at[pl.ds(0, STEP)], buf.at[pl.ds(0, STEP)])])
    lefts = run([copy(left_ref, left)])
    copies += run([copy(a_ref.at[pl.ds(k * STEP, STEP)], buf.at[pl.ds(k * STEP, STEP)]) for k in range(1, n)])
    wait(small)
    c = coup[...]
    middle = exact(exact(c, jnp.sum(s[...], 0), 1, 0), c, 1, 1)
    ms = split(0.5 * (middle + middle.T))
    wait(mid)
    for b in range(cols // WIDE):
        sl = slice(b * WIDE, (b + 1) * WIDE)
        w = wide[:, sl] - three(ms, (right[0, W:, sl], right[1, W:, sl]), 1, 0)
        right[0, :W, sl], right[1, :W, sl] = split(w)
    wait(lefts)
    ends = []
    for k in range(n):
        copies[k].wait()
        lo = k * STEP
        lh = (left[0, lo : lo + STEP], left[1, lo : lo + STEP])
        for b in range(cols // WIDE):
            sl = slice(b * WIDE, (b + 1) * WIDE)
            buf[lo : lo + STEP, sl] -= three(lh, (right[0, :, sl], right[1, :, sl]), 1, 0)
        ends += run([copy(buf.at[pl.ds(lo, STEP)], outs[0].at[pl.ds(lo, STEP)])])
    wait(ends)


def spread(x, n):
    return jnp.broadcast_to(x[None], (n,) + x.shape)


def on_device(matrix):
    rows, cols = matrix.shape
    piece = cols // NR
    half = rows // 2
    r = lax.axis_index("prow")
    c = lax.axis_index("pcol")
    axes = ("prow", "pcol")
    holds_top = (c == 0) | (c == 2) | (c == 4) | (c == 7)
    rc = jnp.stack([r, c, jnp.where(holds_top, 0, half)])
    big = 6 * rows * cols * W

    top, bot = matrix[:half, :W], matrix[half:, :W]
    to1 = lax.ppermute(bot, "pcol", [(0, 1)])
    to2 = lax.ppermute(top, "pcol", [(0, 2)])
    to6 = lax.ppermute(bot, "pcol", [(0, 6)])
    send = jnp.where(c == 0, top, jnp.where(c == 1, to1, jnp.where(c == 2, to2, to6)))
    got = lax.ppermute(send, "pcol", [(0, 7), (1, 3), (2, 4), (6, 5)])
    held = jnp.where((c == 0) | (c == 1) | (c == 2) | (c == 6), send, got)
    other = lax.ppermute(held, "pcol", [(i, i ^ 1) for i in range(NC)])
    owner = [(8 * ((g // NC) % 2) + g % NC) * NC + (g // NC) // 2 for g in range(NR * NC)]
    at = (c % (NC // 2)) * piece
    mine = jnp.where(
        (c < NC // 2) == holds_top,
        lax.dynamic_slice_in_dim(held, at, piece, 0),
        lax.dynamic_slice_in_dim(other, at, piece, 0),
    )
    panel_q = lax.ppermute(mine, axes, list(enumerate(owner)))
    panel_c = lax.all_gather(panel_q, "prow", axis=0, tiled=True)

    half_bufs = [shape(rows, W)]
    small = call(gram_kernel, "gram", 6 * rows * W * W, (rc, held, other), shape(NR, 16, W), half_bufs + [shape(NR, 16, W)], 3)
    small = lax.all_to_all(small, "prow", 0, 0, tiled=True)
    small = spread(jnp.sum(small, 0), NR)
    small = lax.all_to_all(small, "prow", 0, 0, tiled=True)
    msg, linv = call(
        first_kernel,
        "first_pass",
        big,
        (rc, matrix, held, other, small),
        [shape(NR, piece, W), shape(W, W)],
        [shape(rows, cols), shape(rows, W), shape(W, cols), shape(cols, W), shape(NR, 16, W), shape(W, W)],
        4 + rows // STEP + NR,
    )
    msg = lax.all_to_all(msg, "prow", 0, 0, tiled=True)
    coup = call(
        coupling_kernel, "coupling", 8e9, (rc, small, linv), shape(W, W), [shape(NR, 16, W), shape(W, W), shape(W, W)], 3
    )
    msg, coup, panel_c = lax.optimization_barrier((msg, coup, panel_c))
    msg, y_q = call(
        piece_kernel,
        "piece_image",
        msg.size,
        (rc, msg, linv),
        [shape(NR, piece, W), shape(piece, W)],
        [shape(NR, piece, W), shape(W, W), shape(piece, W)],
        2 + NR + 1,
    )
    y_p = lax.ppermute(y_q, axes, [(b, a) for a, b in enumerate(owner)])
    msg = lax.all_to_all(msg, "prow", 0, 0, tiled=True)
    vt = call(
        vectors_kernel,
        "vectors",
        6 * cols * W * W,
        (rc, panel_c, linv),
        shape(2, W, cols, dtype=BF16),
        [shape(cols, W), shape(W, W), shape(2, W, cols, dtype=BF16)],
        3,
    )
    y_r = lax.all_to_all(spread(y_p, NC), "pcol", 0, 0, tiled=True).reshape(rows, W)
    s = call(
        inner_kernel,
        "inner",
        6 * cols * W * W,
        (rc, vt, msg),
        shape(NC, W, W),
        [shape(2, W, cols, dtype=BF16), shape(NR, piece, W), shape(W, W)],
        2 + NC,
    )
    s = lax.all_to_all(s, "pcol", 0, 0, tiled=True)
    left, wide = call(
        sides_kernel,
        "sides",
        12 * (rows + cols) * W * W,
        (rc, held, other, y_r, msg, linv, coup),
        [shape(2, rows, 2 * W, dtype=BF16), shape(W, cols)],
        [
            shape(rows, W),
            shape(rows, W),
            shape(NR, piece, W),
            shape(W, W),
            shape(W, W),
            shape(2, rows, 2 * W, dtype=BF16),
            shape(W, cols),
        ],
        8,
    )
    return call(
        last_kernel,
        "last_pass",
        2 * big,
        (rc, matrix, s, coup, left, wide, vt),
        shape(rows, cols),
        [
            shape(rows, cols),
            shape(NC, W, W),
            shape(W, W),
            shape(2, rows, 2 * W, dtype=BF16),
            shape(W, cols),
            shape(2, 2 * W, cols, dtype=BF16),
        ],
        5 + 2 * (rows // STEP),
    )


def solution(mesh):
    return jax.shard_map(
        on_device, mesh=mesh, in_specs=(P("prow", "pcol"),), out_specs=P("prow", "pcol"), check_vma=False
    )
```

```python
import jax
import jax.numpy as jnp
from jax import lax
from jax.experimental import pallas as pl
from jax.experimental.pallas import tpu as pltpu
from jax.sharding import PartitionSpec as P

W = 128
NR = 16
NC = 8
STEP = 256
WIDE = 512
F32 = jnp.float32
BF16 = jnp.bfloat16
SM = pl.BlockSpec(memory_space=pltpu.SMEM)
HB = pl.BlockSpec(memory_space=pltpu.HBM)


def shape(*dims, dtype=F32):
    return jax.ShapeDtypeStruct(dims, dtype)


def exact(a, b, ca, cb):
    return lax.dot_general(
        a, b, (((ca,), (cb,)), ((), ())), precision=lax.Precision.HIGHEST, preferred_element_type=F32
    )


def split(x):
    hi = x.astype(BF16)
    return hi, (x - hi.astype(F32)).astype(BF16)


def bdot(a, b, ca, cb):
    return lax.dot_general(a, b, (((ca,), (cb,)), ((), ())), preferred_element_type=F32)


def three(a, b, ca, cb):
    (ah, al), (bh, bl) = a, b
    return bdot(ah, bh, ca, cb) + (bdot(ah, bl, ca, cb) + bdot(al, bh, ca, cb))


def dot3(a, b, ca, cb):
    return three(split(a), split(b), ca, cb)


def iota2(dims, dim):
    return lax.broadcasted_iota(jnp.int32, dims, dim)


def run(copies):
    for copy in copies:
        copy.start()
    return copies


def wait(copies):
    for copy in copies:
        copy.wait()


def call(kernel, name, flops, args, outs, scratch, sems):
    single = not isinstance(outs, list)
    out_list = [outs] if single else outs
    size = sum(4 * a.size for a in args[1:]) + sum(4 * o.size for o in out_list)

    def body(*refs):
        n = len(args)
        m = n + len(out_list)
        sem = refs[-1]
        used = []

        def copy(src, dst):
            used.append(None)
            return pltpu.make_async_copy(src, dst, sem.at[len(used) - 1])

        kernel(refs[0], refs[1:n], refs[n:m], refs[m:-1], copy)

    result = pl.pallas_call(
        body,
        in_specs=[SM] + [HB] * (len(args) - 1),
        out_specs=[HB] * len(out_list),
        out_shape=out_list,
        scratch_shapes=[pltpu.VMEM(s.shape, s.dtype) for s in scratch] + [pltpu.SemaphoreType.DMA((sems,))],
        compiler_params=pltpu.CompilerParams(vmem_limit_bytes=60 * 1024 * 1024),
        cost_estimate=pl.CostEstimate(flops=int(flops), bytes_accessed=int(size), transcendentals=0),
        name=name,
    )(*args)
    return result[0] if single else result


def load_panel(rc, held, other, buf, copy):
    half = held.shape[0]
    at = pl.multiple_of(rc[2], half)
    return run([copy(held, buf.at[pl.ds(at, half)]), copy(other, buf.at[pl.ds(half - at, half)])])


def clear_top(rc, buf):
    @pl.when(rc[0] == 0)
    def _():
        buf[:W] = jnp.zeros((W, W), F32)


def gram_kernel(rc, ins, outs, bufs, copy):
    buf, out = bufs
    wait(load_panel(rc, ins[0], ins[1], buf, copy))
    clear_top(rc, buf)
    p = split(buf[...])
    g = three(p, p, 0, 0).reshape(NR, 8, W)
    t = jnp.where(rc[0] == 0, buf[W : 2 * W], 0.0).reshape(NR, 8, W)
    out[...] = jnp.concatenate([g, t], 1)
    wait(run([copy(out, outs[0])]))


def second_kernel(rc, ins, outs, bufs, copy):
    buf, out = bufs
    cols = buf.shape[1]
    wait(run([copy(ins[0].at[pl.ds(W, W)], buf)]))
    for b in range(cols // WIDE):
        sl = slice(b * WIDE, (b + 1) * WIDE)
        out[sl] = buf[:, sl].T
    piece = outs[0].shape[1]
    wait(run([copy(out.at[pl.ds(k * piece, piece)], outs[0].at[k]) for k in range(NR)]))


def first_kernel(rc, ins, outs, bufs, copy):
    a_ref, held, other = ins
    buf, panel, acc, rows_out = bufs
    rows, cols = buf.shape
    n = rows // STEP
    first = load_panel(rc, held, other, panel, copy)
    copies = run([copy(a_ref.at[pl.ds(k * STEP, STEP)], buf.at[pl.ds(k * STEP, STEP)]) for k in range(n)])
    wait(first)
    clear_top(rc, panel)
    ph, plow = split(panel[...])
    both = jnp.concatenate([ph, plow], 1)
    for k in range(n):
        copies[k].wait()
        lo, up = k * STEP, (k + 1) * STEP
        for b in range(cols // WIDE):
            sl = slice(b * WIDE, (b + 1) * WIDE)
            ah, al = split(buf[lo:up, sl])
            x = bdot(both[lo:up], ah, 0, 0)
            x = x[:W] + (x[W:] + bdot(ph[lo:up], al, 0, 0))
            if k == 0:
                acc[:, sl] = x
            elif k < n - 1:
                acc[:, sl] += x
            else:
                rows_out[sl] = (acc[:, sl] + x).T
    piece = outs[0].shape[1]
    wait(run([copy(rows_out.at[pl.ds(k * piece, piece)], outs[0].at[k]) for k in range(NR)]))


def lane(x, k):
    return jnp.broadcast_to(x[:, k : k + 1], (8, W))


def row(x, k):
    return jnp.broadcast_to(x[k : k + 1], (8, W))


def inverse_factor(g):
    lanes = iota2((8, W), 1)
    subs = iota2((8, W), 0)
    tiles = [g[8 * t : 8 * t + 8] for t in range(W // 8)]
    done = []
    for k in range(0, W, 2):
        t0, o = k // 8, k % 8
        top = tiles[t0]
        at0, at1 = lanes == k, lanes == k + 1
        both = at0 | at1
        c0, c1 = lane(top, k), lane(top, k + 1)
        a, b, d = row(c0, o), row(c1, o), row(c1, o + 1)
        r0 = jnp.where(at1, 0.0, jnp.where(at0, 1.0, row(top, o)))
        r1 = jnp.where(at0, 0.0, jnp.where(at1, 1.0, row(top, o + 1)))
        ia = 1.0 / a
        ba = b * ia
        n1 = r1 - ba * r0
        s = d - b * ba
        q1 = n1 * (1.0 / s)
        q0 = r0 * ia - ba * q1
        for t in range(t0, W // 8):
            m = tiles[t]
            if t > t0:
                tiles[t] = jnp.where(both, 0.0, m) - lane(m, k) * q0 - lane(m, k + 1) * q1
            elif o < 6:
                tiles[t] = jnp.where(subs > o + 1, jnp.where(both, 0.0, m) - c0 * q0 - c1 * q1, m)
        if o == 0:
            final = jnp.zeros((8, W), F32)
        final = jnp.where(subs == o, r0 * lax.rsqrt(a), jnp.where(subs == o + 1, n1 * lax.rsqrt(s), final))
        if o == 6:
            done.append(final)
    i, j = iota2((W, W), 0), iota2((W, W), 1)
    return jnp.where(i >= j, jnp.concatenate(done, 0), 0.0)


def factor_kernel(rc, ins, outs, bufs, copy):
    msg, out = bufs
    wait(run([copy(ins[0], msg)]))
    out[...] = inverse_factor(msg[:, :8].reshape(W, W))
    wait(run([copy(out, outs[0])]))


def coupling_kernel(rc, ins, outs, bufs, copy):
    msg, linv, out = bufs
    wait(run([copy(ins[0], msg), copy(ins[1], linv)]))
    i, j = iota2((W, W), 0), iota2((W, W), 1)
    shifted = jnp.where(i == j, 1.0, 0.0) - exact(linv[...], msg[:, 8:].reshape(W, W), 1, 1)
    finv = inverse_factor(exact(shifted, shifted, 0, 0))
    out[...] = exact(finv, exact(finv, shifted, 1, 1), 0, 0)
    wait(run([copy(out, outs[0])]))


def piece_kernel(rc, ins, outs, bufs, copy):
    msg, linv, f, out = bufs
    wait(run([copy(ins[0], msg), copy(ins[1], linv), copy(ins[2].at[0], f)]))
    out[...] = dot3(jnp.sum(msg[...], 0), linv[...], 1, 1) - f[...]
    wait(run([copy(out, outs[0].at[k]) for k in range(NR)] + [copy(out, outs[1])]))


def vectors_kernel(rc, ins, outs, bufs, copy):
    msg, linv, v = bufs
    cols = v.shape[2]
    p = msg.reshape(cols, W)
    wait(run([copy(ins[0], msg), copy(ins[1], linv)]))
    ls = split(linv[...])
    for b in range(cols // WIDE):
        sl = slice(b * WIDE, (b + 1) * WIDE)
        at = iota2((W, WIDE), 1) + (rc[1] * cols + b * WIDE - W)
        x = three(ls, split(p[sl]), 1, 1)
        x = jnp.where(at < 0, 0.0, x) - jnp.where(at == iota2((W, WIDE), 0), 1.0, 0.0)
        v[0, :, sl], v[1, :, sl] = split(x)
    wait(run([copy(v, outs[0])]))


def inner_kernel(rc, ins, outs, bufs, copy):
    v, y, out = bufs
    piece = y.shape[1]
    first = run([copy(ins[0], v), copy(ins[1], y)])
    more = run([copy(ins[2], outs[0].at[k, pl.ds(0, piece)]) for k in range(NC)])
    wait(first)
    out[...] = three((v[0], v[1]), split(y[...].reshape(v.shape[2], W)), 1, 0)
    wait(more + run([copy(out, outs[0].at[k, pl.ds(piece, W)]) for k in range(NC)]))


def sides_kernel(rc, ins, outs, bufs, copy):
    held, other, y_c, linv_ref, coup_ref = ins
    panel, yc, linv, coup, left, wide = bufs
    rows, cols = panel.shape[0], wide.shape[1]
    small = run([copy(linv_ref, linv), copy(coup_ref, coup), copy(y_c, yc)])
    more = load_panel(rc, held, other, panel, copy)
    wait(small)
    ls, cs = split(linv[...]), split(coup[...])
    flat = yc.reshape(cols, W)
    for b in range(cols // WIDE):
        sl = slice(b * WIDE, (b + 1) * WIDE)
        wide[:, sl] = three(cs, split(flat[sl]), 1, 1)
    last = run([copy(wide, outs[1])])
    wait(more)
    clear_top(rc, panel)
    for k in range(rows // STEP):
        sl = slice(k * STEP, (k + 1) * STEP)
        ids = rc[0] * rows + k * STEP + iota2((STEP, W), 0)
        v = three(split(panel[sl]), ls, 1, 1) - jnp.where(ids - W == iota2((STEP, W), 1), 1.0, 0.0)
        left[0, sl], left[1, sl] = split(v)
    wait(last + run([copy(left, outs[0])]))


def last_kernel(rc, ins, outs, bufs, copy):
    a_ref, msg_ref, coup_ref, left_ref, wide_ref, v_ref = ins
    buf, s, coup, yr, left, wide, right = bufs
    rows, cols = buf.shape
    piece = yr.shape[1]
    n = cols // WIDE
    small = run([copy(msg_ref.at[:, pl.ds(piece, W)], s), copy(coup_ref, coup)])
    lefts = run([copy(msg_ref.at[:, pl.ds(0, piece)], yr), copy(left_ref, left.at[:, :, pl.ds(0, W)])])
    mid = run([copy(v_ref, right.at[:, pl.ds(W, W)]), copy(wide_ref, wide)])
    cut = [pl.ds(k * WIDE, WIDE) for k in range(n)]
    copies = run([copy(a_ref.at[:, cut[k]], buf.at[:, cut[k]]) for k in range(n)])
    wait(small)
    cs = split(coup[...])
    middle = three(split(three(cs, split(jnp.sum(s[...], 0)), 1, 0)), cs, 1, 1)
    ms = split(0.5 * (middle + middle.T))
    wait(lefts)
    left[0, :, W:], left[1, :, W:] = split(three(split(yr[...].reshape(rows, W)), cs, 1, 1))
    wait(mid)
    lh, ll = left[0], left[1]
    ends = []
    for k in range(n):
        sl = slice(k * WIDE, (k + 1) * WIDE)
        vh, vl = right[0, W:, sl], right[1, W:, sl]
        wh, wl = split(wide[:, sl] - three(ms, (vh, vl), 1, 0))
        rh = jnp.concatenate([wh, vh], 0)
        rl = jnp.concatenate([wl, vl], 0)
        copies[k].wait()
        buf[:, sl] -= bdot(lh, rh, 1, 0) + (bdot(ll, rh, 1, 0) + bdot(lh, rl, 1, 0))
        ends += run([copy(buf.at[:, cut[k]], outs[0].at[:, cut[k]])])
    wait(ends)


def spread(x, n):
    return jnp.broadcast_to(x[None], (n,) + x.shape)


def on_device(matrix):
    rows, cols = matrix.shape
    piece = cols // NR
    half = rows // 2
    r = lax.axis_index("prow")
    c = lax.axis_index("pcol")
    axes = ("prow", "pcol")
    holds_top = (c == 0) | (c == 2) | (c == 4) | (c == 7)
    rc = jnp.stack([r, c, jnp.where(holds_top, 0, half)])
    big = 6 * rows * cols * W

    top, bot = matrix[:half, :W], matrix[half:, :W]
    to1 = lax.ppermute(bot, "pcol", [(0, 1)])
    to2 = lax.ppermute(top, "pcol", [(0, 2)])
    to6 = lax.ppermute(bot, "pcol", [(0, 6)])
    f_msg = call(
        second_kernel, "second", W, (rc, matrix), shape(NR, piece, W), [shape(W, cols), shape(cols, W)], 1 + NR
    )
    f_msg = lax.all_to_all(f_msg, "prow", 0, 0, tiled=True)
    send = jnp.where(c == 0, top, jnp.where(c == 1, to1, jnp.where(c == 2, to2, to6)))
    got = lax.ppermute(send, "pcol", [(0, 7), (1, 3), (2, 4), (6, 5)])
    held = jnp.where((c == 0) | (c == 1) | (c == 2) | (c == 6), send, got)
    other = lax.ppermute(held, "pcol", [(i, i ^ 1) for i in range(NC)])
    owner = [(8 * ((g // NC) % 2) + g % NC) * NC + (g // NC) // 2 for g in range(NR * NC)]
    at = (c % (NC // 2)) * piece
    mine = jnp.where(
        (c < NC // 2) == holds_top,
        lax.dynamic_slice_in_dim(held, at, piece, 0),
        lax.dynamic_slice_in_dim(other, at, piece, 0),
    )
    panel_q = lax.ppermute(mine, axes, list(enumerate(owner)))
    half_bufs = [shape(rows, W)]
    small = call(gram_kernel, "gram", 6 * rows * W * W, (rc, held, other), shape(NR, 16, W), half_bufs + [shape(NR, 16, W)], 3)
    small, f_msg, panel_q = lax.optimization_barrier((small, f_msg, panel_q))
    small = lax.all_to_all(small, "prow", 0, 0, tiled=True)
    panel_c = lax.all_to_all(spread(panel_q, NR), "prow", 0, 0, tiled=True)
    msg = call(
        first_kernel,
        "first_pass",
        big,
        (rc, matrix, held, other),
        shape(NR, piece, W),
        [shape(rows, cols), shape(rows, W), shape(W, cols), shape(cols, W)],
        2 + rows // STEP + NR,
    )
    small = spread(jnp.sum(small, 0), NR)
    small, msg = lax.optimization_barrier((small, msg))
    small = lax.all_to_all(small, "prow", 0, 0, tiled=True)
    msg, panel_c = lax.optimization_barrier((msg, panel_c))
    msg = lax.all_to_all(msg, "prow", 0, 0, tiled=True)
    linv = call(factor_kernel, "factor", 8e9, (rc, small), shape(W, W), [shape(NR, 16, W), shape(W, W)], 2)
    msg, y_q = call(
        piece_kernel,
        "piece_image",
        msg.size,
        (rc, msg, linv, f_msg),
        [shape(NR, piece, W), shape(piece, W)],
        [shape(NR, piece, W), shape(W, W), shape(piece, W), shape(piece, W)],
        3 + NR + 1,
    )
    y_q, small = lax.optimization_barrier((y_q, small))
    y_p = lax.ppermute(y_q, axes, [(b, a) for a, b in enumerate(owner)])
    msg = lax.all_to_all(msg, "prow", 0, 0, tiled=True)
    coup = call(
        coupling_kernel, "coupling", 8e9, (rc, small, linv), shape(W, W), [shape(NR, 16, W), shape(W, W), shape(W, W)], 3
    )
    vt = call(
        vectors_kernel,
        "vectors",
        6 * cols * W * W,
        (rc, panel_c, linv),
        shape(2, W, cols, dtype=BF16),
        [shape(NR, piece, W), shape(W, W), shape(2, W, cols, dtype=BF16)],
        3,
    )
    end = call(
        inner_kernel,
        "inner",
        6 * cols * W * W,
        (rc, vt, msg, y_p),
        shape(NC, piece + W, W),
        [shape(2, W, cols, dtype=BF16), shape(NR, piece, W), shape(W, W)],
        2 + 2 * NC,
    )
    end = lax.all_to_all(end, "pcol", 0, 0, tiled=True)
    left, wide = call(
        sides_kernel,
        "sides",
        12 * (rows + cols) * W * W,
        (rc, held, other, msg, linv, coup),
        [shape(2, rows, W, dtype=BF16), shape(W, cols)],
        [
            shape(rows, W),
            shape(NR, piece, W),
            shape(W, W),
            shape(W, W),
            shape(2, rows, W, dtype=BF16),
            shape(W, cols),
        ],
        7,
    )
    return call(
        last_kernel,
        "last_pass",
        2 * big,
        (rc, matrix, end, coup, left, wide, vt),
        shape(rows, cols),
        [
            shape(rows, cols),
            shape(NC, W, W),
            shape(W, W),
            shape(NC, piece, W),
            shape(2, rows, 2 * W, dtype=BF16),
            shape(W, cols),
            shape(2, 2 * W, cols, dtype=BF16),
        ],
        6 + 2 * (cols // WIDE),
    )


def solution(mesh):
    return jax.shard_map(
        on_device, mesh=mesh, in_specs=(P("prow", "pcol"),), out_specs=P("prow", "pcol"), check_vma=False
    )
```

```python
import jax
import jax.numpy as jnp
from jax import lax
from jax.experimental import pallas as pl
from jax.experimental.pallas import tpu as pltpu
from jax.sharding import PartitionSpec as P

W = 128
NR = 16
NC = 8
STEP = 256
WIDE = 512
F32 = jnp.float32
BF16 = jnp.bfloat16
SM = pl.BlockSpec(memory_space=pltpu.SMEM)
HB = pl.BlockSpec(memory_space=pltpu.HBM)


def shape(*dims, dtype=F32):
    return jax.ShapeDtypeStruct(dims, dtype)


def exact(a, b, ca, cb):
    return lax.dot_general(
        a, b, (((ca,), (cb,)), ((), ())), precision=lax.Precision.HIGHEST, preferred_element_type=F32
    )


def split(x):
    hi = x.astype(BF16)
    return hi, (x - hi.astype(F32)).astype(BF16)


def bdot(a, b, ca, cb):
    return lax.dot_general(a, b, (((ca,), (cb,)), ((), ())), preferred_element_type=F32)


def three(a, b, ca, cb):
    (ah, al), (bh, bl) = a, b
    return bdot(ah, bh, ca, cb) + (bdot(ah, bl, ca, cb) + bdot(al, bh, ca, cb))


def dot3(a, b, ca, cb):
    return three(split(a), split(b), ca, cb)


def iota2(dims, dim):
    return lax.broadcasted_iota(jnp.int32, dims, dim)


def run(copies):
    for copy in copies:
        copy.start()
    return copies


def wait(copies):
    for copy in copies:
        copy.wait()


def call(kernel, name, flops, args, outs, scratch, sems):
    single = not isinstance(outs, list)
    out_list = [outs] if single else outs
    size = sum(4 * a.size for a in args[1:]) + sum(4 * o.size for o in out_list)

    def body(*refs):
        n = len(args)
        m = n + len(out_list)
        sem = refs[-1]
        used = []

        def copy(src, dst):
            used.append(None)
            return pltpu.make_async_copy(src, dst, sem.at[len(used) - 1])

        kernel(refs[0], refs[1:n], refs[n:m], refs[m:-1], copy)

    result = pl.pallas_call(
        body,
        in_specs=[SM] + [HB] * (len(args) - 1),
        out_specs=[HB] * len(out_list),
        out_shape=out_list,
        scratch_shapes=[pltpu.VMEM(s.shape, s.dtype) for s in scratch] + [pltpu.SemaphoreType.DMA((sems,))],
        compiler_params=pltpu.CompilerParams(vmem_limit_bytes=60 * 1024 * 1024),
        cost_estimate=pl.CostEstimate(flops=int(flops), bytes_accessed=int(size), transcendentals=0),
        name=name,
    )(*args)
    return result[0] if single else result


def load_panel(rc, held, other, buf, copy):
    half = held.shape[0]
    at = pl.multiple_of(rc[2], half)
    return run([copy(held, buf.at[pl.ds(at, half)]), copy(other, buf.at[pl.ds(half - at, half)])])


def clear_top(rc, buf):
    @pl.when(rc[0] == 0)
    def _():
        buf[:W] = jnp.zeros((W, W), F32)


def gram_kernel(rc, ins, outs, bufs, copy):
    buf, out = bufs
    wait(load_panel(rc, ins[0], ins[1], buf, copy))
    clear_top(rc, buf)
    p = split(buf[...])
    g = three(p, p, 0, 0).reshape(NR, 8, W)
    t = jnp.where(rc[0] == 0, buf[W : 2 * W], 0.0).reshape(NR, 8, W)
    out[...] = jnp.concatenate([g, t], 1)
    wait(run([copy(out, outs[0])]))


def mix_kernel(rc, ins, outs, bufs, copy):
    msg, p, small = bufs
    piece, n = p.shape[0], small.shape[0]
    first = run([copy(ins[0], msg)])
    wait(run([copy(ins[1], p)]))
    more = run([copy(p, outs[0].at[k, pl.ds(0, piece)]) for k in range(NR)])
    wait(first)
    small[...] = jnp.sum(msg[...], 0)
    wait(more + run([copy(small, outs[0].at[k, pl.ds(piece, n)]) for k in range(NR)]))


def second_kernel(rc, ins, outs, bufs, copy):
    buf, out = bufs
    cols = buf.shape[1]
    wait(run([copy(ins[0].at[pl.ds(W, W)], buf)]))
    for b in range(cols // WIDE):
        sl = slice(b * WIDE, (b + 1) * WIDE)
        out[sl] = buf[:, sl].T
    piece = outs[0].shape[1]
    wait(run([copy(out.at[pl.ds(k * piece, piece)], outs[0].at[k]) for k in range(NR)]))


def first_kernel(rc, ins, outs, bufs, copy):
    a_ref, held, other = ins
    buf, panel, acc, rows_out = bufs
    rows, cols = buf.shape
    n = rows // STEP
    first = load_panel(rc, held, other, panel, copy)
    copies = run([copy(a_ref.at[pl.ds(k * STEP, STEP)], buf.at[pl.ds(k * STEP, STEP)]) for k in range(n)])
    wait(first)
    clear_top(rc, panel)
    ph, plow = split(panel[...])
    both = jnp.concatenate([ph, plow], 1)
    for k in range(n):
        copies[k].wait()
        lo, up = k * STEP, (k + 1) * STEP
        for b in range(cols // WIDE):
            sl = slice(b * WIDE, (b + 1) * WIDE)
            ah, al = split(buf[lo:up, sl])
            x = bdot(both[lo:up], ah, 0, 0)
            x = x[:W] + (x[W:] + bdot(ph[lo:up], al, 0, 0))
            if k == 0:
                acc[:, sl] = x
            elif k < n - 1:
                acc[:, sl] += x
            else:
                rows_out[sl] = (acc[:, sl] + x).T
    piece = outs[0].shape[1]
    wait(run([copy(rows_out.at[pl.ds(k * piece, piece)], outs[0].at[k]) for k in range(NR)]))


def lane(x, k):
    return jnp.broadcast_to(x[:, k : k + 1], (8, W))


def row(x, k):
    return jnp.broadcast_to(x[k : k + 1], (8, W))


def inverse_factor(g):
    lanes = iota2((8, W), 1)
    subs = iota2((8, W), 0)
    tiles = [g[8 * t : 8 * t + 8] for t in range(W // 8)]
    done = []
    for k in range(0, W, 2):
        t0, o = k // 8, k % 8
        top = tiles[t0]
        at0, at1 = lanes == k, lanes == k + 1
        both = at0 | at1
        c0, c1 = lane(top, k), lane(top, k + 1)
        a, b, d = row(c0, o), row(c1, o), row(c1, o + 1)
        r0 = jnp.where(at1, 0.0, jnp.where(at0, 1.0, row(top, o)))
        r1 = jnp.where(at0, 0.0, jnp.where(at1, 1.0, row(top, o + 1)))
        ia = 1.0 / a
        ba = b * ia
        n1 = r1 - ba * r0
        s = d - b * ba
        q1 = n1 * (1.0 / s)
        q0 = r0 * ia - ba * q1
        for t in range(t0, W // 8):
            m = tiles[t]
            if t > t0:
                tiles[t] = jnp.where(both, 0.0, m) - lane(m, k) * q0 - lane(m, k + 1) * q1
            elif o < 6:
                tiles[t] = jnp.where(subs > o + 1, jnp.where(both, 0.0, m) - c0 * q0 - c1 * q1, m)
        if o == 0:
            final = jnp.zeros((8, W), F32)
        final = jnp.where(subs == o, r0 * lax.rsqrt(a), jnp.where(subs == o + 1, n1 * lax.rsqrt(s), final))
        if o == 6:
            done.append(final)
    i, j = iota2((W, W), 0), iota2((W, W), 1)
    return jnp.where(i >= j, jnp.concatenate(done, 0), 0.0)


def factor_kernel(rc, ins, outs, bufs, copy):
    msg, out = bufs
    wait(run([copy(ins[0].at[:, pl.ds(ins[0].shape[1] - 16, 8)], msg)]))
    out[...] = inverse_factor(msg[...].reshape(W, W))
    wait(run([copy(out, outs[0])]))


def coupling_kernel(rc, ins, outs, bufs, copy):
    msg, linv, out = bufs
    wait(run([copy(ins[0].at[:, pl.ds(ins[0].shape[1] - 8, 8)], msg), copy(ins[1], linv)]))
    i, j = iota2((W, W), 0), iota2((W, W), 1)
    shifted = jnp.where(i == j, 1.0, 0.0) - exact(linv[...], msg[...].reshape(W, W), 1, 1)
    finv = inverse_factor(exact(shifted, shifted, 0, 0))
    out[...] = exact(finv, exact(finv, shifted, 1, 1), 0, 0)
    wait(run([copy(out, outs[0])]))


def piece_kernel(rc, ins, outs, bufs, copy):
    msg, linv, f, out = bufs
    wait(run([copy(ins[0], msg), copy(ins[1], linv), copy(ins[2].at[0], f)]))
    out[...] = dot3(jnp.sum(msg[...], 0), linv[...], 1, 1) - f[...]
    wait(run([copy(out, outs[0].at[k]) for k in range(NR)] + [copy(out, outs[1])]))


def vectors_kernel(rc, ins, outs, bufs, copy):
    msg, linv, v = bufs
    cols = v.shape[2]
    p = msg.reshape(cols, W)
    wait(run([copy(ins[0].at[:, pl.ds(0, msg.shape[1])], msg), copy(ins[1], linv)]))
    ls = split(linv[...])
    for b in range(cols // WIDE):
        sl = slice(b * WIDE, (b + 1) * WIDE)
        at = iota2((W, WIDE), 1) + (rc[1] * cols + b * WIDE - W)
        x = three(ls, split(p[sl]), 1, 1)
        x = jnp.where(at < 0, 0.0, x) - jnp.where(at == iota2((W, WIDE), 0), 1.0, 0.0)
        v[0, :, sl], v[1, :, sl] = split(x)
    wait(run([copy(v, outs[0])]))


def inner_kernel(rc, ins, outs, bufs, copy):
    v, y, out, mine = bufs
    piece = y.shape[1]
    first = run([copy(ins[0], v), copy(ins[1], y)])
    wait(run([copy(ins[2], mine)]))
    more = run([copy(mine, outs[0].at[k, pl.ds(0, piece)]) for k in range(NC)])
    wait(first)
    out[...] = three((v[0], v[1]), split(y[...].reshape(v.shape[2], W)), 1, 0)
    wait(more + run([copy(out, outs[0].at[k, pl.ds(piece, W)]) for k in range(NC)]))


def sides_kernel(rc, ins, outs, bufs, copy):
    held, other, y_c, linv_ref, coup_ref = ins
    panel, yc, linv, coup, left, wide = bufs
    rows, cols = panel.shape[0], wide.shape[1]
    small = run([copy(linv_ref, linv), copy(coup_ref, coup), copy(y_c, yc)])
    more = load_panel(rc, held, other, panel, copy)
    wait(small)
    ls, cs = split(linv[...]), split(coup[...])
    flat = yc.reshape(cols, W)
    for b in range(cols // WIDE):
        sl = slice(b * WIDE, (b + 1) * WIDE)
        wide[:, sl] = three(cs, split(flat[sl]), 1, 1)
    last = run([copy(wide, outs[1])])
    wait(more)
    clear_top(rc, panel)
    for k in range(rows // STEP):
        sl = slice(k * STEP, (k + 1) * STEP)
        ids = rc[0] * rows + k * STEP + iota2((STEP, W), 0)
        v = three(split(panel[sl]), ls, 1, 1) - jnp.where(ids - W == iota2((STEP, W), 1), 1.0, 0.0)
        left[0, sl], left[1, sl] = split(v)
    wait(last + run([copy(left, outs[0])]))


def last_kernel(rc, ins, outs, bufs, copy):
    a_ref, msg_ref, coup_ref, left_ref, wide_ref, v_ref = ins
    buf, s, coup, yr, left, wide, right = bufs
    rows, cols = buf.shape
    piece = yr.shape[1]
    n = cols // WIDE
    small = run([copy(msg_ref.at[:, pl.ds(piece, W)], s), copy(coup_ref, coup)])
    lefts = run([copy(msg_ref.at[:, pl.ds(0, piece)], yr), copy(left_ref, left.at[:, :, pl.ds(0, W)])])
    mid = run([copy(v_ref, right.at[:, pl.ds(W, W)]), copy(wide_ref, wide)])
    cut = [pl.ds(k * WIDE, WIDE) for k in range(n)]
    copies = run([copy(a_ref.at[:, cut[k]], buf.at[:, cut[k]]) for k in range(n)])
    wait(small)
    cs = split(coup[...])
    middle = three(split(three(cs, split(jnp.sum(s[...], 0)), 1, 0)), cs, 1, 1)
    ms = split(0.5 * (middle + middle.T))
    wait(lefts)
    left[0, :, W:], left[1, :, W:] = split(three(split(yr[...].reshape(rows, W)), cs, 1, 1))
    wait(mid)
    lh, ll = left[0], left[1]
    ends = []
    for k in range(n):
        sl = slice(k * WIDE, (k + 1) * WIDE)
        vh, vl = right[0, W:, sl], right[1, W:, sl]
        wh, wl = split(wide[:, sl] - three(ms, (vh, vl), 1, 0))
        rh = jnp.concatenate([wh, vh], 0)
        rl = jnp.concatenate([wl, vl], 0)
        copies[k].wait()
        buf[:, sl] -= bdot(lh, rh, 1, 0) + (bdot(ll, rh, 1, 0) + bdot(lh, rl, 1, 0))
        ends += run([copy(buf.at[:, cut[k]], outs[0].at[:, cut[k]])])
    wait(ends)


def on_device(matrix):
    rows, cols = matrix.shape
    piece = cols // NR
    half = rows // 2
    r = lax.axis_index("prow")
    c = lax.axis_index("pcol")
    axes = ("prow", "pcol")
    holds_top = (c == 0) | (c == 2) | (c == 4) | (c == 7)
    rc = jnp.stack([r, c, jnp.where(holds_top, 0, half)])
    big = 6 * rows * cols * W

    top, bot = matrix[:half, :W], matrix[half:, :W]
    to1 = lax.ppermute(bot, "pcol", [(0, 1)])
    to2 = lax.ppermute(top, "pcol", [(0, 2)])
    to6 = lax.ppermute(bot, "pcol", [(0, 6)])
    f_msg = call(
        second_kernel, "second", W, (rc, matrix), shape(NR, piece, W), [shape(W, cols), shape(cols, W)], 1 + NR
    )
    f_msg = lax.all_to_all(f_msg, "prow", 0, 0, tiled=True)
    send = jnp.where(c == 0, top, jnp.where(c == 1, to1, jnp.where(c == 2, to2, to6)))
    got = lax.ppermute(send, "pcol", [(0, 7), (1, 3), (2, 4), (6, 5)])
    held = jnp.where((c == 0) | (c == 1) | (c == 2) | (c == 6), send, got)
    other = lax.ppermute(held, "pcol", [(i, i ^ 1) for i in range(NC)])
    owner = [(8 * ((g // NC) % 2) + g % NC) * NC + (g // NC) // 2 for g in range(NR * NC)]
    at = (c % (NC // 2)) * piece
    mine = jnp.where(
        (c < NC // 2) == holds_top,
        lax.dynamic_slice_in_dim(held, at, piece, 0),
        lax.dynamic_slice_in_dim(other, at, piece, 0),
    )
    panel_q = lax.ppermute(mine, axes, list(enumerate(owner)))
    half_bufs = [shape(rows, W)]
    small = call(gram_kernel, "gram", 6 * rows * W * W, (rc, held, other), shape(NR, 16, W), half_bufs + [shape(NR, 16, W)], 3)
    small, f_msg = lax.optimization_barrier((small, f_msg))
    small = lax.all_to_all(small, "prow", 0, 0, tiled=True)
    small = call(
        mix_kernel,
        "mix",
        NR * 16 * W,
        (rc, small, panel_q),
        shape(NR, piece + 16, W),
        [shape(NR, 16, W), shape(piece, W), shape(16, W)],
        2 + 2 * NR,
    )
    small, held, other = lax.optimization_barrier((small, held, other))
    small = lax.all_to_all(small, "prow", 0, 0, tiled=True)
    msg = call(
        first_kernel,
        "first_pass",
        big,
        (rc, matrix, held, other),
        shape(NR, piece, W),
        [shape(rows, cols), shape(rows, W), shape(W, cols), shape(cols, W)],
        2 + rows // STEP + NR,
    )
    msg = lax.all_to_all(msg, "prow", 0, 0, tiled=True)
    linv = call(factor_kernel, "factor", 8e9, (rc, small), shape(W, W), [shape(NR, 8, W), shape(W, W)], 2)
    msg, y_q = call(
        piece_kernel,
        "piece_image",
        msg.size,
        (rc, msg, linv, f_msg),
        [shape(NR, piece, W), shape(piece, W)],
        [shape(NR, piece, W), shape(W, W), shape(piece, W), shape(piece, W)],
        3 + NR + 1,
    )
    y_q, small = lax.optimization_barrier((y_q, small))
    y_p = lax.ppermute(y_q, axes, [(b, a) for a, b in enumerate(owner)])
    msg = lax.all_to_all(msg, "prow", 0, 0, tiled=True)
    coup = call(
        coupling_kernel, "coupling", 8e9, (rc, small, linv), shape(W, W), [shape(NR, 8, W), shape(W, W), shape(W, W)], 3
    )
    vt = call(
        vectors_kernel,
        "vectors",
        6 * cols * W * W,
        (rc, small, linv),
        shape(2, W, cols, dtype=BF16),
        [shape(NR, piece, W), shape(W, W), shape(2, W, cols, dtype=BF16)],
        3,
    )
    end = call(
        inner_kernel,
        "inner",
        6 * cols * W * W,
        (rc, vt, msg, y_p),
        shape(NC, piece + W, W),
        [shape(2, W, cols, dtype=BF16), shape(NR, piece, W), shape(W, W), shape(piece, W)],
        3 + 2 * NC,
    )
    end = lax.all_to_all(end, "pcol", 0, 0, tiled=True)
    left, wide = call(
        sides_kernel,
        "sides",
        12 * (rows + cols) * W * W,
        (rc, held, other, msg, linv, coup),
        [shape(2, rows, W, dtype=BF16), shape(W, cols)],
        [
            shape(rows, W),
            shape(NR, piece, W),
            shape(W, W),
            shape(W, W),
            shape(2, rows, W, dtype=BF16),
            shape(W, cols),
        ],
        7,
    )
    return call(
        last_kernel,
        "last_pass",
        2 * big,
        (rc, matrix, end, coup, left, wide, vt),
        shape(rows, cols),
        [
            shape(rows, cols),
            shape(NC, W, W),
            shape(W, W),
            shape(NC, piece, W),
            shape(2, rows, 2 * W, dtype=BF16),
            shape(W, cols),
            shape(2, 2 * W, cols, dtype=BF16),
        ],
        6 + 2 * (cols // WIDE),
    )


def solution(mesh):
    return jax.shard_map(
        on_device, mesh=mesh, in_specs=(P("prow", "pcol"),), out_specs=P("prow", "pcol"), check_vma=False
    )
```

```python
import jax
import jax.numpy as jnp
from jax import lax
from jax.experimental import pallas as pl
from jax.experimental.pallas import tpu as pltpu
from jax.sharding import PartitionSpec as P

W = 128
NR = 16
NC = 8
STEP = 256
WIDE = 512
LIMITS = {"gram": 20, "mix": 20, "factor": 20, "second": 52, "first_pass": 52}
F32 = jnp.float32
BF16 = jnp.bfloat16
SM = pl.BlockSpec(memory_space=pltpu.SMEM)
HB = pl.BlockSpec(memory_space=pltpu.HBM)


def shape(*dims, dtype=F32):
    return jax.ShapeDtypeStruct(dims, dtype)


def exact(a, b, ca, cb):
    return lax.dot_general(
        a, b, (((ca,), (cb,)), ((), ())), precision=lax.Precision.HIGHEST, preferred_element_type=F32
    )


def split(x):
    hi = x.astype(BF16)
    return hi, (x - hi.astype(F32)).astype(BF16)


def bdot(a, b, ca, cb):
    return lax.dot_general(a, b, (((ca,), (cb,)), ((), ())), preferred_element_type=F32)


def three(a, b, ca, cb):
    (ah, al), (bh, bl) = a, b
    return bdot(ah, bh, ca, cb) + (bdot(ah, bl, ca, cb) + bdot(al, bh, ca, cb))


def dot3(a, b, ca, cb):
    return three(split(a), split(b), ca, cb)


def iota2(dims, dim):
    return lax.broadcasted_iota(jnp.int32, dims, dim)


def run(copies):
    for copy in copies:
        copy.start()
    return copies


def wait(copies):
    for copy in copies:
        copy.wait()


def call(kernel, name, flops, args, outs, scratch, sems):
    limit = LIMITS.get(name, 60)
    single = not isinstance(outs, list)
    out_list = [outs] if single else outs
    size = sum(4 * a.size for a in args[1:]) + sum(4 * o.size for o in out_list)

    def body(*refs):
        n = len(args)
        m = n + len(out_list)
        sem = refs[-1]
        used = []

        def copy(src, dst):
            used.append(None)
            return pltpu.make_async_copy(src, dst, sem.at[len(used) - 1])

        kernel(refs[0], refs[1:n], refs[n:m], refs[m:-1], copy)

    result = pl.pallas_call(
        body,
        in_specs=[SM] + [pl.BlockSpec(memory_space=pl.ANY)] * (len(args) - 1),
        out_specs=[HB] * len(out_list),
        out_shape=out_list,
        scratch_shapes=[pltpu.VMEM(s.shape, s.dtype) for s in scratch] + [pltpu.SemaphoreType.DMA((sems,))],
        compiler_params=pltpu.CompilerParams(vmem_limit_bytes=limit * 1024 * 1024),
        cost_estimate=pl.CostEstimate(flops=int(flops), bytes_accessed=int(size), transcendentals=0),
        name=name,
    )(*args)
    return result[0] if single else result


def load_panel(rc, held, other, buf, copy):
    half = held.shape[0]
    at = pl.multiple_of(rc[2], half)
    return run([copy(held, buf.at[pl.ds(at, half)]), copy(other, buf.at[pl.ds(half - at, half)])])


def clear_top(rc, buf):
    @pl.when(rc[0] == 0)
    def _():
        buf[:W] = jnp.zeros((W, W), F32)


def gram_kernel(rc, ins, outs, bufs, copy):
    buf, out = bufs
    wait(load_panel(rc, ins[0], ins[1], buf, copy))
    clear_top(rc, buf)
    p = split(buf[...])
    g = three(p, p, 0, 0).reshape(NR, 8, W)
    t = jnp.where(rc[0] == 0, buf[W : 2 * W], 0.0).reshape(NR, 8, W)
    out[...] = jnp.concatenate([g, t], 1)
    wait(run([copy(out, outs[0])]))


def mix_kernel(rc, ins, outs, bufs, copy):
    msg, p, small = bufs
    piece, n = p.shape[0], small.shape[0]
    first = run([copy(ins[0], msg)])
    wait(run([copy(ins[1], p)]))
    more = run([copy(p, outs[0].at[k, pl.ds(0, piece)]) for k in range(NR)])
    wait(first)
    small[...] = jnp.sum(msg[...], 0)
    wait(more + run([copy(small, outs[0].at[k, pl.ds(piece, n)]) for k in range(NR)]))


def second_kernel(rc, ins, outs, bufs, copy):
    buf, out = bufs
    cols = buf.shape[1]
    wait(run([copy(ins[0].at[pl.ds(W, W)], buf)]))
    for b in range(cols // WIDE):
        sl = slice(b * WIDE, (b + 1) * WIDE)
        out[sl] = buf[:, sl].T
    piece = outs[0].shape[1]
    wait(run([copy(out.at[pl.ds(k * piece, piece)], outs[0].at[k]) for k in range(NR)]))


def first_kernel(rc, ins, outs, bufs, copy):
    a_ref, held, other = ins
    buf, panel, acc, rows_out = bufs
    rows, cols = buf.shape
    n = rows // STEP
    first = load_panel(rc, held, other, panel, copy)
    copies = run([copy(a_ref.at[pl.ds(k * STEP, STEP)], buf.at[pl.ds(k * STEP, STEP)]) for k in range(n)])
    wait(first)
    clear_top(rc, panel)
    ph, plow = split(panel[...])
    both = jnp.concatenate([ph, plow], 1)
    for k in range(n):
        copies[k].wait()
        lo, up = k * STEP, (k + 1) * STEP
        for b in range(cols // WIDE):
            sl = slice(b * WIDE, (b + 1) * WIDE)
            ah, al = split(buf[lo:up, sl])
            x = bdot(both[lo:up], ah, 0, 0)
            x = x[:W] + (x[W:] + bdot(ph[lo:up], al, 0, 0))
            if k == 0:
                acc[:, sl] = x
            elif k < n - 1:
                acc[:, sl] += x
            else:
                rows_out[sl] = (acc[:, sl] + x).T
    piece = outs[0].shape[1]
    wait(run([copy(rows_out.at[pl.ds(k * piece, piece)], outs[0].at[k]) for k in range(NR)]))


def lane(x, k):
    return jnp.broadcast_to(x[:, k : k + 1], (8, W))


def row(x, k):
    return jnp.broadcast_to(x[k : k + 1], (8, W))


def inverse_factor(g):
    lanes = iota2((8, W), 1)
    subs = iota2((8, W), 0)
    tiles = [g[8 * t : 8 * t + 8] for t in range(W // 8)]
    done = []
    for k in range(0, W, 2):
        t0, o = k // 8, k % 8
        top = tiles[t0]
        at0, at1 = lanes == k, lanes == k + 1
        both = at0 | at1
        c0, c1 = lane(top, k), lane(top, k + 1)
        a, b, d = row(c0, o), row(c1, o), row(c1, o + 1)
        r0 = jnp.where(at1, 0.0, jnp.where(at0, 1.0, row(top, o)))
        r1 = jnp.where(at0, 0.0, jnp.where(at1, 1.0, row(top, o + 1)))
        ia = 1.0 / a
        ba = b * ia
        n1 = r1 - ba * r0
        s = d - b * ba
        q1 = n1 * (1.0 / s)
        q0 = r0 * ia - ba * q1
        for t in range(t0, W // 8):
            m = tiles[t]
            if t > t0:
                tiles[t] = jnp.where(both, 0.0, m) - lane(m, k) * q0 - lane(m, k + 1) * q1
            elif o < 6:
                tiles[t] = jnp.where(subs > o + 1, jnp.where(both, 0.0, m) - c0 * q0 - c1 * q1, m)
        if o == 0:
            final = jnp.zeros((8, W), F32)
        final = jnp.where(subs == o, r0 * lax.rsqrt(a), jnp.where(subs == o + 1, n1 * lax.rsqrt(s), final))
        if o == 6:
            done.append(final)
    i, j = iota2((W, W), 0), iota2((W, W), 1)
    return jnp.where(i >= j, jnp.concatenate(done, 0), 0.0)


def factor_kernel(rc, ins, outs, bufs, copy):
    msg, out = bufs
    wait(run([copy(ins[0].at[:, pl.ds(ins[0].shape[1] - 16, 8)], msg)]))
    out[...] = inverse_factor(msg[...].reshape(W, W))
    wait(run([copy(out, outs[0])]))


def coupling_kernel(rc, ins, outs, bufs, copy):
    msg, linv, out = bufs
    wait(run([copy(ins[0].at[:, pl.ds(ins[0].shape[1] - 8, 8)], msg), copy(ins[1], linv)]))
    i, j = iota2((W, W), 0), iota2((W, W), 1)
    shifted = jnp.where(i == j, 1.0, 0.0) - exact(linv[...], msg[...].reshape(W, W), 1, 1)
    finv = inverse_factor(exact(shifted, shifted, 0, 0))
    out[...] = exact(finv, exact(finv, shifted, 1, 1), 0, 0)
    wait(run([copy(out, outs[0])]))


def piece_kernel(rc, ins, outs, bufs, copy):
    msg, linv, f, out = bufs
    wait(run([copy(ins[0], msg), copy(ins[1], linv), copy(ins[2].at[0], f)]))
    out[...] = dot3(jnp.sum(msg[...], 0), linv[...], 1, 1) - f[...]
    wait(run([copy(out, outs[0].at[k]) for k in range(NR)] + [copy(out, outs[1])]))


def vectors_kernel(rc, ins, outs, bufs, copy):
    msg, linv, v, panel, left = bufs
    cols, rows = v.shape[2], panel.shape[0]
    more = load_panel(rc, ins[2], ins[3], panel, copy)
    p = msg.reshape(cols, W)
    wait(run([copy(ins[0].at[:, pl.ds(0, msg.shape[1])], msg), copy(ins[1], linv)]))
    ls = split(linv[...])
    for b in range(cols // WIDE):
        sl = slice(b * WIDE, (b + 1) * WIDE)
        at = iota2((W, WIDE), 1) + (rc[1] * cols + b * WIDE - W)
        x = three(ls, split(p[sl]), 1, 1)
        x = jnp.where(at < 0, 0.0, x) - jnp.where(at == iota2((W, WIDE), 0), 1.0, 0.0)
        v[0, :, sl], v[1, :, sl] = split(x)
    last = run([copy(v, outs[0])])
    wait(more)
    clear_top(rc, panel)
    for k in range(rows // STEP):
        sl = slice(k * STEP, (k + 1) * STEP)
        ids = rc[0] * rows + k * STEP + iota2((STEP, W), 0)
        x = three(split(panel[sl]), ls, 1, 1) - jnp.where(ids - W == iota2((STEP, W), 1), 1.0, 0.0)
        left[0, sl], left[1, sl] = split(x)
    wait(last + run([copy(left, outs[1])]))


def inner_kernel(rc, ins, outs, bufs, copy):
    v, y, out, mine = bufs
    piece = y.shape[1]
    first = run([copy(ins[0], v), copy(ins[1], y)])
    wait(run([copy(ins[2], mine)]))
    more = run([copy(mine, outs[0].at[k, pl.ds(0, piece)]) for k in range(NC)])
    wait(first)
    out[...] = three((v[0], v[1]), split(y[...].reshape(v.shape[2], W)), 1, 0)
    wait(more + run([copy(out, outs[0].at[k, pl.ds(piece, W)]) for k in range(NC)]))


def sides_kernel(rc, ins, outs, bufs, copy):
    yc, coup, wide = bufs
    cols = wide.shape[1]
    wait(run([copy(ins[0], yc), copy(ins[1], coup)]))
    cs = split(coup[...])
    flat = yc.reshape(cols, W)
    for b in range(cols // WIDE):
        sl = slice(b * WIDE, (b + 1) * WIDE)
        wide[:, sl] = three(cs, split(flat[sl]), 1, 1)
    wait(run([copy(wide, outs[0])]))


def last_kernel(rc, ins, outs, bufs, copy):
    a_ref, msg_ref, coup_ref, left_ref, wide_ref, v_ref = ins
    buf, s, coup, yr, left, wide, right = bufs
    rows, cols = buf.shape
    piece = yr.shape[1]
    n = cols // WIDE
    small = run([copy(msg_ref.at[:, pl.ds(piece, W)], s), copy(coup_ref, coup)])
    lefts = run([copy(msg_ref.at[:, pl.ds(0, piece)], yr)])
    for i, part in enumerate((0, 1, 0)):
        lefts += run([copy(left_ref.at[part], left.at[:, pl.ds(2 * i * W, W)])])
    mid = run([copy(v_ref, right), copy(wide_ref, wide)])
    cut = [pl.ds(k * WIDE, WIDE) for k in range(n)]
    copies = run([copy(a_ref.at[:, cut[k]], buf.at[:, cut[k]]) for k in range(n)])
    wait(small)
    cs = split(coup[...])
    middle = three(split(three(cs, split(jnp.sum(s[...], 0)), 1, 0)), cs, 1, 1)
    ms = split(0.5 * (middle + middle.T))
    wait(lefts)
    high, low = split(three(split(yr[...].reshape(rows, W)), cs, 1, 1))
    for i, part in enumerate((high, low, high)):
        left[:, (2 * i + 1) * W : (2 * i + 2) * W] = part
    wait(mid)
    ends = []
    for k in range(n):
        sl = slice(k * WIDE, (k + 1) * WIDE)
        vh, vl = right[0, :, sl], right[1, :, sl]
        wh, wl = split(wide[:, sl] - three(ms, (vh, vl), 1, 0))
        three_parts = jnp.concatenate([wh, vh, wh, vh, wl, vl], 0)
        copies[k].wait()
        buf[:, sl] -= bdot(left[...], three_parts, 1, 0)
        ends += run([copy(buf.at[:, cut[k]], outs[0].at[:, cut[k]])])
    wait(ends)


def on_device(matrix):
    rows, cols = matrix.shape
    piece = cols // NR
    half = rows // 2
    r = lax.axis_index("prow")
    c = lax.axis_index("pcol")
    axes = ("prow", "pcol")
    holds_top = (c == 0) | (c == 2) | (c == 4) | (c == 7)
    rc = jnp.stack([r, c, jnp.where(holds_top, 0, half)])
    big = 6 * rows * cols * W

    top, bot = matrix[:half, :W], matrix[half:, :W]
    to1 = lax.ppermute(bot, "pcol", [(0, 1)])
    to2 = lax.ppermute(top, "pcol", [(0, 2)])
    to6 = lax.ppermute(bot, "pcol", [(0, 6)])
    f_msg = call(
        second_kernel, "second", W, (rc, matrix), shape(NR, piece, W), [shape(W, cols), shape(cols, W)], 1 + NR
    )
    send = jnp.where(c == 0, top, jnp.where(c == 1, to1, jnp.where(c == 2, to2, to6)))
    f_msg, send = lax.optimization_barrier((f_msg, send))
    f_msg = lax.all_to_all(f_msg, "prow", 0, 0, tiled=True)
    got = lax.ppermute(send, "pcol", [(0, 7), (1, 3), (2, 4), (6, 5)])
    held = jnp.where((c == 0) | (c == 1) | (c == 2) | (c == 6), send, got)
    other = lax.ppermute(held, "pcol", [(i, i ^ 1) for i in range(NC)])
    owner = [(8 * ((g // NC) % 2) + g % NC) * NC + (g // NC) // 2 for g in range(NR * NC)]

    at = (c % (NC // 2)) * piece
    mine = jnp.where(
        (c < NC // 2) == holds_top,
        lax.dynamic_slice_in_dim(held, at, piece, 0),
        lax.dynamic_slice_in_dim(other, at, piece, 0),
    )
    panel_q = lax.ppermute(mine, axes, list(enumerate(owner)))
    half_bufs = [shape(rows, W)]
    small = call(gram_kernel, "gram", 6 * rows * W * W, (rc, held, other), shape(NR, 16, W), half_bufs + [shape(NR, 16, W)], 3)
    small, f_msg = lax.optimization_barrier((small, f_msg))
    small = lax.all_to_all(small, "prow", 0, 0, tiled=True)
    small = call(
        mix_kernel,
        "mix",
        NR * 16 * W,
        (rc, small, panel_q),
        shape(NR, piece + 16, W),
        [shape(NR, 16, W), shape(piece, W), shape(16, W)],
        2 + 2 * NR,
    )
    small, held, other = lax.optimization_barrier((small, held, other))
    small = lax.all_to_all(small, "prow", 0, 0, tiled=True)
    msg = call(
        first_kernel,
        "first_pass",
        big,
        (rc, matrix, held, other),
        shape(NR, piece, W),
        [shape(rows, cols), shape(rows, W), shape(W, cols), shape(cols, W)],
        2 + rows // STEP + NR,
    )
    msg = lax.all_to_all(msg, "prow", 0, 0, tiled=True)
    linv = call(factor_kernel, "factor", 8e9, (rc, small), shape(W, W), [shape(NR, 8, W), shape(W, W)], 2)
    msg, y_q = call(
        piece_kernel,
        "piece_image",
        msg.size,
        (rc, msg, linv, f_msg),
        [shape(NR, piece, W), shape(piece, W)],
        [shape(NR, piece, W), shape(W, W), shape(piece, W), shape(piece, W)],
        3 + NR + 1,
    )
    y_q, small = lax.optimization_barrier((y_q, small))
    y_p = lax.ppermute(y_q, axes, [(b, a) for a, b in enumerate(owner)])
    msg = lax.all_to_all(msg, "prow", 0, 0, tiled=True)
    coup = call(
        coupling_kernel, "coupling", 8e9, (rc, small, linv), shape(W, W), [shape(NR, 8, W), shape(W, W), shape(W, W)], 3
    )
    vt, left = call(
        vectors_kernel,
        "vectors",
        6 * (rows + cols) * W * W,
        (rc, small, linv, held, other),
        [shape(2, W, cols, dtype=BF16), shape(2, rows, W, dtype=BF16)],
        [
            shape(NR, piece, W),
            shape(W, W),
            shape(2, W, cols, dtype=BF16),
            shape(rows, W),
            shape(2, rows, W, dtype=BF16),
        ],
        6,
    )
    end = call(
        inner_kernel,
        "inner",
        6 * cols * W * W,
        (rc, vt, msg, y_p),
        shape(NC, piece + W, W),
        [shape(2, W, cols, dtype=BF16), shape(NR, piece, W), shape(W, W), shape(piece, W)],
        3 + 2 * NC,
    )
    end = lax.all_to_all(end, "pcol", 0, 0, tiled=True)
    wide = call(
        sides_kernel,
        "sides",
        6 * cols * W * W,
        (rc, msg, coup),
        shape(W, cols),
        [shape(NR, piece, W), shape(W, W), shape(W, cols)],
        3,
    )
    return call(
        last_kernel,
        "last_pass",
        2 * big,
        (rc, matrix, end, coup, left, wide, vt),
        shape(rows, cols),
        [
            shape(rows, cols),
            shape(NC, W, W),
            shape(W, W),
            shape(NC, piece, W),
            shape(rows, 6 * W, dtype=BF16),
            shape(W, cols),
            shape(2, W, cols, dtype=BF16),
        ],
        8 + 2 * (cols // WIDE),
    )


def solution(mesh):
    return jax.shard_map(
        on_device, mesh=mesh, in_specs=(P("prow", "pcol"),), out_specs=P("prow", "pcol"), check_vma=False
    )
```

```python
import jax
import jax.numpy as jnp
from jax import lax
from jax.experimental import pallas as pl
from jax.experimental.pallas import tpu as pltpu
from jax.sharding import PartitionSpec as P

W = 128
NR = 16
NC = 8
STEP = 256
WIDE = 512
LIMITS = {"gram": 20, "mix": 20, "factor": 20, "coupling": 20, "piece_image": 20, "vectors": 20, "second": 52, "first_pass": 52}
F32 = jnp.float32
BF16 = jnp.bfloat16
SM = pl.BlockSpec(memory_space=pltpu.SMEM)
HB = pl.BlockSpec(memory_space=pltpu.HBM)


def shape(*dims, dtype=F32):
    return jax.ShapeDtypeStruct(dims, dtype)


def exact(a, b, ca, cb):
    return lax.dot_general(
        a, b, (((ca,), (cb,)), ((), ())), precision=lax.Precision.HIGHEST, preferred_element_type=F32
    )


def split(x):
    hi = x.astype(BF16)
    return hi, (x - hi.astype(F32)).astype(BF16)


def bdot(a, b, ca, cb):
    return lax.dot_general(a, b, (((ca,), (cb,)), ((), ())), preferred_element_type=F32)


def three(a, b, ca, cb):
    (ah, al), (bh, bl) = a, b
    return bdot(ah, bh, ca, cb) + (bdot(ah, bl, ca, cb) + bdot(al, bh, ca, cb))


def dot3(a, b, ca, cb):
    return three(split(a), split(b), ca, cb)


def iota2(dims, dim):
    return lax.broadcasted_iota(jnp.int32, dims, dim)


def run(copies):
    for copy in copies:
        copy.start()
    return copies


def wait(copies):
    for copy in copies:
        copy.wait()


def call(kernel, name, flops, args, outs, scratch, sems):
    limit = LIMITS.get(name, 60)
    single = not isinstance(outs, list)
    out_list = [outs] if single else outs
    size = sum(4 * a.size for a in args[1:]) + sum(4 * o.size for o in out_list)

    def body(*refs):
        n = len(args)
        m = n + len(out_list)
        sem = refs[-1]
        used = []

        def copy(src, dst):
            used.append(None)
            return pltpu.make_async_copy(src, dst, sem.at[len(used) - 1])

        kernel(refs[0], refs[1:n], refs[n:m], refs[m:-1], copy)

    result = pl.pallas_call(
        body,
        in_specs=[SM] + [pl.BlockSpec(memory_space=pl.ANY)] * (len(args) - 1),
        out_specs=[HB] * len(out_list),
        out_shape=out_list,
        scratch_shapes=[pltpu.VMEM(s.shape, s.dtype) for s in scratch] + [pltpu.SemaphoreType.DMA((sems,))],
        compiler_params=pltpu.CompilerParams(vmem_limit_bytes=limit * 1024 * 1024),
        cost_estimate=pl.CostEstimate(flops=int(flops), bytes_accessed=int(size), transcendentals=0),
        name=name,
    )(*args)
    return result[0] if single else result


def load_panel(rc, held, other, buf, copy):
    half = held.shape[0]
    at = pl.multiple_of(rc[2], half)
    return run([copy(held, buf.at[pl.ds(at, half)]), copy(other, buf.at[pl.ds(half - at, half)])])


def clear_top(rc, buf):
    @pl.when(rc[0] == 0)
    def _():
        buf[:W] = jnp.zeros((W, W), F32)


def gram_kernel(rc, ins, outs, bufs, copy):
    buf, out = bufs
    wait(load_panel(rc, ins[0], ins[1], buf, copy))
    clear_top(rc, buf)
    p = split(buf[...])
    g = three(p, p, 0, 0).reshape(NR, 8, W)
    t = jnp.where(rc[0] == 0, buf[W : 2 * W], 0.0).reshape(NR, 8, W)
    out[...] = jnp.concatenate([g, t], 1)
    wait(run([copy(out, outs[0])]))


def mix_kernel(rc, ins, outs, bufs, copy):
    msg, small = bufs
    wait(run([copy(ins[0], msg)]))
    small[...] = jnp.sum(msg[...], 0)
    wait(run([copy(small, outs[0].at[k]) for k in range(NR)]))


def second_kernel(rc, ins, outs, bufs, copy):
    buf, out = bufs
    cols = buf.shape[1]
    wait(run([copy(ins[0].at[pl.ds(W, W)], buf)]))
    for b in range(cols // WIDE):
        sl = slice(b * WIDE, (b + 1) * WIDE)
        out[sl] = buf[:, sl].T
    piece = outs[0].shape[1]
    wait(run([copy(out.at[pl.ds(k * piece, piece)], outs[0].at[k]) for k in range(NR)]))


def first_kernel(rc, ins, outs, bufs, copy):
    a_ref, held, other, mine_ref = ins
    buf, panel, acc, rows_out, mine = bufs
    piece = mine.shape[0]
    rows, cols = buf.shape
    n = rows // STEP
    first = load_panel(rc, held, other, panel, copy)
    copies = run([copy(a_ref.at[pl.ds(k * STEP, STEP)], buf.at[pl.ds(k * STEP, STEP)]) for k in range(n)])
    early = run([copy(mine_ref, mine)])
    wait(first + early)
    more = run([copy(mine, outs[0].at[k, pl.ds(piece, piece)]) for k in range(NR)])
    clear_top(rc, panel)
    ph, plow = split(panel[...])
    both = jnp.concatenate([ph, plow], 1)
    for k in range(n):
        copies[k].wait()
        lo, up = k * STEP, (k + 1) * STEP
        for b in range(cols // WIDE):
            sl = slice(b * WIDE, (b + 1) * WIDE)
            ah, al = split(buf[lo:up, sl])
            x = bdot(both[lo:up], ah, 0, 0)
            x = x[:W] + (x[W:] + bdot(ph[lo:up], al, 0, 0))
            if k == 0:
                acc[:, sl] = x
            elif k < n - 1:
                acc[:, sl] += x
            else:
                rows_out[sl] = (acc[:, sl] + x).T
    wait(more + run([copy(rows_out.at[pl.ds(k * piece, piece)], outs[0].at[k, pl.ds(0, piece)]) for k in range(NR)]))


def lane(x, k):
    return jnp.broadcast_to(x[:, k : k + 1], (8, W))


def row(x, k):
    return jnp.broadcast_to(x[k : k + 1], (8, W))


def inverse_factor(g):
    lanes = iota2((8, W), 1)
    subs = iota2((8, W), 0)
    tiles = [g[8 * t : 8 * t + 8] for t in range(W // 8)]
    done = []
    for k in range(0, W, 2):
        t0, o = k // 8, k % 8
        top = tiles[t0]
        at0, at1 = lanes == k, lanes == k + 1
        both = at0 | at1
        c0, c1 = lane(top, k), lane(top, k + 1)
        a, b, d = row(c0, o), row(c1, o), row(c1, o + 1)
        r0 = jnp.where(at1, 0.0, jnp.where(at0, 1.0, row(top, o)))
        r1 = jnp.where(at0, 0.0, jnp.where(at1, 1.0, row(top, o + 1)))
        ia = 1.0 / a
        ba = b * ia
        n1 = r1 - ba * r0
        s = d - b * ba
        q1 = n1 * (1.0 / s)
        q0 = r0 * ia - ba * q1
        for t in range(t0, W // 8):
            m = tiles[t]
            if t > t0:
                tiles[t] = jnp.where(both, 0.0, m) - lane(m, k) * q0 - lane(m, k + 1) * q1
            elif o < 6:
                tiles[t] = jnp.where(subs > o + 1, jnp.where(both, 0.0, m) - c0 * q0 - c1 * q1, m)
        if o == 0:
            final = jnp.zeros((8, W), F32)
        final = jnp.where(subs == o, r0 * lax.rsqrt(a), jnp.where(subs == o + 1, n1 * lax.rsqrt(s), final))
        if o == 6:
            done.append(final)
    i, j = iota2((W, W), 0), iota2((W, W), 1)
    return jnp.where(i >= j, jnp.concatenate(done, 0), 0.0)


def factor_kernel(rc, ins, outs, bufs, copy):
    msg, out = bufs
    wait(run([copy(ins[0].at[:, pl.ds(ins[0].shape[1] - 16, 8)], msg)]))
    out[...] = inverse_factor(msg[...].reshape(W, W))
    wait(run([copy(out, outs[0])]))


def coupling_kernel(rc, ins, outs, bufs, copy):
    msg, linv, out = bufs
    wait(run([copy(ins[0].at[:, pl.ds(ins[0].shape[1] - 8, 8)], msg), copy(ins[1], linv)]))
    i, j = iota2((W, W), 0), iota2((W, W), 1)
    shifted = jnp.where(i == j, 1.0, 0.0) - exact(linv[...], msg[...].reshape(W, W), 1, 1)
    finv = inverse_factor(exact(shifted, shifted, 0, 0))
    out[...] = exact(finv, exact(finv, shifted, 1, 1), 0, 0)
    wait(run([copy(out, outs[0])]))


def piece_kernel(rc, ins, outs, bufs, copy):
    msg, linv, f, out = bufs
    wait(run([copy(ins[0].at[:, pl.ds(0, msg.shape[1])], msg), copy(ins[1], linv), copy(ins[2], f)]))
    out[...] = dot3(jnp.sum(msg[...], 0), linv[...], 1, 1) - f[...]
    wait(run([copy(out, outs[0].at[k]) for k in range(NR)] + [copy(out, outs[1])]))


def vectors_kernel(rc, ins, outs, bufs, copy):
    msg, linv, v, panel, left = bufs
    cols, rows = v.shape[2], panel.shape[0]
    more = load_panel(rc, ins[2], ins[3], panel, copy)
    p = msg.reshape(cols, W)
    wait(run([copy(ins[0].at[:, pl.ds(msg.shape[1], msg.shape[1])], msg), copy(ins[1], linv)]))
    ls = split(linv[...])
    for b in range(cols // WIDE):
        sl = slice(b * WIDE, (b + 1) * WIDE)
        at = iota2((W, WIDE), 1) + (rc[1] * cols + b * WIDE - W)
        x = three(ls, split(p[sl]), 1, 1)
        x = jnp.where(at < 0, 0.0, x) - jnp.where(at == iota2((W, WIDE), 0), 1.0, 0.0)
        v[0, :, sl], v[1, :, sl] = split(x)
    last = run([copy(v, outs[0])])
    wait(more)
    clear_top(rc, panel)
    for k in range(rows // STEP):
        sl = slice(k * STEP, (k + 1) * STEP)
        ids = rc[0] * rows + k * STEP + iota2((STEP, W), 0)
        x = three(split(panel[sl]), ls, 1, 1) - jnp.where(ids - W == iota2((STEP, W), 1), 1.0, 0.0)
        left[0, sl], left[1, sl] = split(x)
    wait(last + run([copy(left, outs[1])]))


def inner_kernel(rc, ins, outs, bufs, copy):
    v, y, out, mine = bufs
    piece = y.shape[1]
    first = run([copy(ins[0], v), copy(ins[1], y)])
    wait(run([copy(ins[2], mine)]))
    more = run([copy(mine, outs[0].at[k, pl.ds(0, piece)]) for k in range(NC)])
    wait(first)
    out[...] = three((v[0], v[1]), split(y[...].reshape(v.shape[2], W)), 1, 0)
    wait(more + run([copy(out, outs[0].at[k, pl.ds(piece, W)]) for k in range(NC)]))


def sides_kernel(rc, ins, outs, bufs, copy):
    yc, coup, wide = bufs
    cols = wide.shape[1]
    wait(run([copy(ins[0], yc), copy(ins[1], coup)]))
    cs = split(coup[...])
    flat = yc.reshape(cols, W)
    for b in range(cols // WIDE):
        sl = slice(b * WIDE, (b + 1) * WIDE)
        wide[:, sl] = three(cs, split(flat[sl]), 1, 1)
    wait(run([copy(wide, outs[0])]))


def last_kernel(rc, ins, outs, bufs, copy):
    a_ref, msg_ref, coup_ref, left_ref, wide_ref, v_ref = ins
    buf, s, coup, yr, left, wide, right = bufs
    rows, cols = buf.shape
    piece = yr.shape[1]
    n = cols // WIDE
    small = run([copy(msg_ref.at[:, pl.ds(piece, W)], s), copy(coup_ref, coup)])
    lefts = run([copy(msg_ref.at[:, pl.ds(0, piece)], yr)])
    for i, part in enumerate((0, 1, 0)):
        lefts += run([copy(left_ref.at[part], left.at[:, pl.ds(2 * i * W, W)])])
    mid = run([copy(v_ref, right), copy(wide_ref, wide)])
    cut = [pl.ds(k * WIDE, WIDE) for k in range(n)]
    copies = run([copy(a_ref.at[:, cut[k]], buf.at[:, cut[k]]) for k in range(n)])
    wait(small)
    cs = split(coup[...])
    middle = three(split(three(cs, split(jnp.sum(s[...], 0)), 1, 0)), cs, 1, 1)
    ms = split(0.5 * (middle + middle.T))
    wait(lefts)
    high, low = split(three(split(yr[...].reshape(rows, W)), cs, 1, 1))
    for i, part in enumerate((high, low, high)):
        left[:, (2 * i + 1) * W : (2 * i + 2) * W] = part
    wait(mid)
    ends = []
    for k in range(n):
        sl = slice(k * WIDE, (k + 1) * WIDE)
        vh, vl = right[0, :, sl], right[1, :, sl]
        wh, wl = split(wide[:, sl] - three(ms, (vh, vl), 1, 0))
        three_parts = jnp.concatenate([wh, vh, wh, vh, wl, vl], 0)
        copies[k].wait()
        buf[:, sl] -= bdot(left[...], three_parts, 1, 0)
        ends += run([copy(buf.at[:, cut[k]], outs[0].at[:, cut[k]])])
    wait(ends)


def on_device(matrix):
    rows, cols = matrix.shape
    piece = cols // NR
    half = rows // 2
    r = lax.axis_index("prow")
    c = lax.axis_index("pcol")
    axes = ("prow", "pcol")
    holds_top = (c == 0) | (c == 2) | (c == 4) | (c == 7)
    rc = jnp.stack([r, c, jnp.where(holds_top, 0, half)])
    big = 6 * rows * cols * W

    top, bot = matrix[:half, :W], matrix[half:, :W]
    to1 = lax.ppermute(bot, "pcol", [(0, 1)])
    to2 = lax.ppermute(top, "pcol", [(0, 2)])
    to6 = lax.ppermute(bot, "pcol", [(0, 6)])
    f_msg = call(
        second_kernel, "second", W, (rc, matrix), shape(NR, piece, W), [shape(W, cols), shape(cols, W)], 1 + NR
    )
    send = jnp.where(c == 0, top, jnp.where(c == 1, to1, jnp.where(c == 2, to2, to6)))
    f_msg, send = lax.optimization_barrier((f_msg, send))
    f_msg = lax.all_to_all(f_msg, "prow", 0, 0, tiled=True)
    got = lax.ppermute(send, "pcol", [(0, 7), (1, 3), (2, 4), (6, 5)])
    held = jnp.where((c == 0) | (c == 1) | (c == 2) | (c == 6), send, got)
    other = lax.ppermute(held, "pcol", [(i, i ^ 1) for i in range(NC)])
    owner = [(8 * ((g // NC) % 2) + g % NC) * NC + (g // NC) // 2 for g in range(NR * NC)]

    at = (c % (NC // 2)) * piece
    mine = jnp.where(
        (c < NC // 2) == holds_top,
        lax.dynamic_slice_in_dim(held, at, piece, 0),
        lax.dynamic_slice_in_dim(other, at, piece, 0),
    )
    panel_q = lax.ppermute(mine, axes, list(enumerate(owner)))
    half_bufs = [shape(rows, W)]
    small = call(gram_kernel, "gram", 6 * rows * W * W, (rc, held, other), shape(NR, 16, W), half_bufs + [shape(NR, 16, W)], 3)
    small, f_q = lax.optimization_barrier((small, f_msg[0]))
    small = lax.all_to_all(small, "prow", 0, 0, tiled=True)
    small = call(
        mix_kernel,
        "mix",
        NR * 16 * W,
        (rc, small),
        shape(NR, 16, W),
        [shape(NR, 16, W), shape(16, W)],
        1 + NR,
    )
    small, held, other = lax.optimization_barrier((small, held, other))
    small = lax.all_to_all(small, "prow", 0, 0, tiled=True)
    msg = call(
        first_kernel,
        "first_pass",
        big,
        (rc, matrix, held, other, panel_q),
        shape(NR, 2 * piece, W),
        [shape(rows, cols), shape(rows, W), shape(W, cols), shape(cols, W), shape(piece, W)],
        3 + rows // STEP + 2 * NR,
    )
    msg = lax.all_to_all(msg, "prow", 0, 0, tiled=True)
    linv = call(factor_kernel, "factor", 8e9, (rc, small), shape(W, W), [shape(NR, 8, W), shape(W, W)], 2)
    coup = call(
        coupling_kernel, "coupling", 8e9, (rc, small, linv), shape(W, W), [shape(NR, 8, W), shape(W, W), shape(W, W)], 3
    )
    sums, linv, coup = lax.optimization_barrier((msg, linv, coup))
    msg, y_q = call(
        piece_kernel,
        "piece_image",
        msg.size,
        (rc, sums, linv, f_q),
        [shape(NR, piece, W), shape(piece, W)],
        [shape(NR, piece, W), shape(W, W), shape(piece, W), shape(piece, W)],
        3 + NR + 1,
    )
    y_p = lax.ppermute(y_q, axes, [(b, a) for a, b in enumerate(owner)])
    msg = lax.all_to_all(msg, "prow", 0, 0, tiled=True)
    vt, left = call(
        vectors_kernel,
        "vectors",
        6 * (rows + cols) * W * W,
        (rc, sums, linv, held, other),
        [shape(2, W, cols, dtype=BF16), shape(2, rows, W, dtype=BF16)],
        [
            shape(NR, piece, W),
            shape(W, W),
            shape(2, W, cols, dtype=BF16),
            shape(rows, W),
            shape(2, rows, W, dtype=BF16),
        ],
        6,
    )
    end = call(
        inner_kernel,
        "inner",
        6 * cols * W * W,
        (rc, vt, msg, y_p),
        shape(NC, piece + W, W),
        [shape(2, W, cols, dtype=BF16), shape(NR, piece, W), shape(W, W), shape(piece, W)],
        3 + 2 * NC,
    )
    end = lax.all_to_all(end, "pcol", 0, 0, tiled=True)
    wide = call(
        sides_kernel,
        "sides",
        6 * cols * W * W,
        (rc, msg, coup),
        shape(W, cols),
        [shape(NR, piece, W), shape(W, W), shape(W, cols)],
        3,
    )
    return call(
        last_kernel,
        "last_pass",
        2 * big,
        (rc, matrix, end, coup, left, wide, vt),
        shape(rows, cols),
        [
            shape(rows, cols),
            shape(NC, W, W),
            shape(W, W),
            shape(NC, piece, W),
            shape(rows, 6 * W, dtype=BF16),
            shape(W, cols),
            shape(2, W, cols, dtype=BF16),
        ],
        8 + 2 * (cols // WIDE),
    )


def solution(mesh):
    return jax.shard_map(
        on_device, mesh=mesh, in_specs=(P("prow", "pcol"),), out_specs=P("prow", "pcol"), check_vma=False
    )
```

```python
import jax
import jax.numpy as jnp
from jax import lax
from jax.experimental import pallas as pl
from jax.experimental.pallas import tpu as pltpu
from jax.sharding import PartitionSpec as P

W = 128
NR = 16
NC = 8
STEP = 256
WIDE = 512
LIMITS = {"gram": 20, "mix": 20, "factor": 20, "coupling": 20, "piece_image": 20, "vectors": 20, "second": 52, "first_pass": 52}
F32 = jnp.float32
BF16 = jnp.bfloat16
SM = pl.BlockSpec(memory_space=pltpu.SMEM)
HB = pl.BlockSpec(memory_space=pltpu.HBM)


def shape(*dims, dtype=F32):
    return jax.ShapeDtypeStruct(dims, dtype)


def exact(a, b, ca, cb):
    return lax.dot_general(
        a, b, (((ca,), (cb,)), ((), ())), precision=lax.Precision.HIGHEST, preferred_element_type=F32
    )


def split(x):
    hi = x.astype(BF16)
    return hi, (x - hi.astype(F32)).astype(BF16)


def bdot(a, b, ca, cb):
    return lax.dot_general(a, b, (((ca,), (cb,)), ((), ())), preferred_element_type=F32)


def three(a, b, ca, cb):
    (ah, al), (bh, bl) = a, b
    return bdot(ah, bh, ca, cb) + (bdot(ah, bl, ca, cb) + bdot(al, bh, ca, cb))


def dot3(a, b, ca, cb):
    return three(split(a), split(b), ca, cb)


def iota2(dims, dim):
    return lax.broadcasted_iota(jnp.int32, dims, dim)


def run(copies):
    for copy in copies:
        copy.start()
    return copies


def wait(copies):
    for copy in copies:
        copy.wait()


def call(kernel, name, flops, args, outs, scratch, sems):
    limit = LIMITS.get(name, 60)
    single = not isinstance(outs, list)
    out_list = [outs] if single else outs
    size = sum(4 * a.size for a in args[1:]) + sum(4 * o.size for o in out_list)

    def body(*refs):
        n = len(args)
        m = n + len(out_list)
        sem = refs[-1]
        used = []

        def copy(src, dst):
            used.append(None)
            return pltpu.make_async_copy(src, dst, sem.at[len(used) - 1])

        kernel(refs[0], refs[1:n], refs[n:m], refs[m:-1], copy)

    result = pl.pallas_call(
        body,
        in_specs=[SM] + [pl.BlockSpec(memory_space=pl.ANY)] * (len(args) - 1),
        out_specs=[HB] * len(out_list),
        out_shape=out_list,
        scratch_shapes=[pltpu.VMEM(s.shape, s.dtype) for s in scratch] + [pltpu.SemaphoreType.DMA((sems,))],
        compiler_params=pltpu.CompilerParams(vmem_limit_bytes=limit * 1024 * 1024),
        cost_estimate=pl.CostEstimate(flops=int(flops), bytes_accessed=int(size), transcendentals=0),
        name=name,
    )(*args)
    return result[0] if single else result


def load_panel(rc, held, other, buf, copy):
    half = held.shape[0]
    at = pl.multiple_of(rc[2], half)
    return run([copy(held, buf.at[pl.ds(at, half)]), copy(other, buf.at[pl.ds(half - at, half)])])


def clear_top(rc, buf):
    @pl.when(rc[0] == 0)
    def _():
        buf[:W] = jnp.zeros((W, W), F32)


def gram_kernel(rc, ins, outs, bufs, copy):
    buf, out = bufs
    wait(load_panel(rc, ins[0], ins[1], buf, copy))
    clear_top(rc, buf)
    p = split(buf[...])
    g = three(p, p, 0, 0).reshape(NR, 8, W)
    t = jnp.where(rc[0] == 0, buf[W : 2 * W], 0.0).reshape(NR, 8, W)
    out[...] = jnp.concatenate([g, t], 1)
    wait(run([copy(out, outs[0])]))


def mix_kernel(rc, ins, outs, bufs, copy):
    msg, small = bufs
    wait(run([copy(ins[0], msg)]))
    small[...] = jnp.sum(msg[...], 0)
    wait(run([copy(small, outs[0].at[k]) for k in range(NR)]))


def second_kernel(rc, ins, outs, bufs, copy):
    buf, out = bufs
    cols = buf.shape[1]
    wait(run([copy(ins[0].at[pl.ds(W, W)], buf)]))
    for b in range(cols // WIDE):
        sl = slice(b * WIDE, (b + 1) * WIDE)
        out[sl] = buf[:, sl].T
    piece = outs[0].shape[1]
    wait(run([copy(out.at[pl.ds(k * piece, piece)], outs[0].at[k]) for k in range(NR)]))


def first_kernel(rc, ins, outs, bufs, copy):
    a_ref, held, other, mine_ref = ins
    buf, panel, acc, rows_out, mine = bufs
    piece = mine.shape[0]
    rows, cols = buf.shape
    n = rows // STEP
    first = load_panel(rc, held, other, panel, copy)
    copies = run([copy(a_ref.at[pl.ds(k * STEP, STEP)], buf.at[pl.ds(k * STEP, STEP)]) for k in range(n)])
    early = run([copy(mine_ref, mine)])
    wait(first + early)
    more = run([copy(mine, outs[0].at[k, pl.ds(piece, piece)]) for k in range(NR)])
    clear_top(rc, panel)
    ph, plow = split(panel[...])
    both = jnp.concatenate([ph, plow], 1)
    for k in range(n):
        copies[k].wait()
        lo, up = k * STEP, (k + 1) * STEP
        for b in range(cols // WIDE):
            sl = slice(b * WIDE, (b + 1) * WIDE)
            ah, al = split(buf[lo:up, sl])
            x = bdot(both[lo:up], ah, 0, 0)
            x = x[:W] + (x[W:] + bdot(ph[lo:up], al, 0, 0))
            if k == 0:
                acc[:, sl] = x
            elif k < n - 1:
                acc[:, sl] += x
            else:
                rows_out[sl] = (acc[:, sl] + x).T
    wait(more + run([copy(rows_out.at[pl.ds(k * piece, piece)], outs[0].at[k, pl.ds(0, piece)]) for k in range(NR)]))


def lane(x, k):
    return jnp.broadcast_to(x[:, k : k + 1], (8, W))


def row(x, k):
    return jnp.broadcast_to(x[k : k + 1], (8, W))


def inverse_factor(g):
    lanes = iota2((8, W), 1)
    subs = iota2((8, W), 0)
    tiles = [g[8 * t : 8 * t + 8] for t in range(W // 8)]
    done = []
    for k in range(0, W, 2):
        t0, o = k // 8, k % 8
        top = tiles[t0]
        at0, at1 = lanes == k, lanes == k + 1
        both = at0 | at1
        c0, c1 = lane(top, k), lane(top, k + 1)
        a, b, d = row(c0, o), row(c1, o), row(c1, o + 1)
        r0 = jnp.where(at1, 0.0, jnp.where(at0, 1.0, row(top, o)))
        r1 = jnp.where(at0, 0.0, jnp.where(at1, 1.0, row(top, o + 1)))
        ia = 1.0 / a
        ba = b * ia
        n1 = r1 - ba * r0
        s = d - b * ba
        q1 = n1 * (1.0 / s)
        q0 = r0 * ia - ba * q1
        for t in range(t0, W // 8):
            m = tiles[t]
            if t > t0:
                tiles[t] = jnp.where(both, 0.0, m) - lane(m, k) * q0 - lane(m, k + 1) * q1
            elif o < 6:
                tiles[t] = jnp.where(subs > o + 1, jnp.where(both, 0.0, m) - c0 * q0 - c1 * q1, m)
        if o == 0:
            final = jnp.zeros((8, W), F32)
        final = jnp.where(subs == o, r0 * lax.rsqrt(a), jnp.where(subs == o + 1, n1 * lax.rsqrt(s), final))
        if o == 6:
            done.append(final)
    i, j = iota2((W, W), 0), iota2((W, W), 1)
    return jnp.where(i >= j, jnp.concatenate(done, 0), 0.0)


def factor_kernel(rc, ins, outs, bufs, copy):
    msg, out = bufs
    wait(run([copy(ins[0].at[:, pl.ds(ins[0].shape[1] - 16, 8)], msg)]))
    out[...] = inverse_factor(msg[...].reshape(W, W))
    wait(run([copy(out, outs[0])]))


def coupling_kernel(rc, ins, outs, bufs, copy):
    msg, linv, out = bufs
    wait(run([copy(ins[0].at[:, pl.ds(ins[0].shape[1] - 8, 8)], msg), copy(ins[1], linv)]))
    i, j = iota2((W, W), 0), iota2((W, W), 1)
    shifted = jnp.where(i == j, 1.0, 0.0) - exact(linv[...], msg[...].reshape(W, W), 1, 1)
    finv = inverse_factor(exact(shifted, shifted, 0, 0))
    out[...] = exact(finv, exact(finv, shifted, 1, 1), 0, 0)
    wait(run([copy(out, outs[0])]))


def piece_kernel(rc, ins, outs, bufs, copy):
    msg, linv, f, out = bufs
    wait(run([copy(ins[0].at[:, pl.ds(0, msg.shape[1])], msg), copy(ins[1], linv), copy(ins[2], f)]))
    out[...] = dot3(jnp.sum(msg[...], 0), linv[...], 1, 1) - f[...]
    wait(run([copy(out, outs[0].at[k]) for k in range(NR)] + [copy(out, outs[1])]))


def vectors_kernel(rc, ins, outs, bufs, copy):
    msg, linv, v, panel, left = bufs
    cols, rows = v.shape[2], panel.shape[0]
    more = load_panel(rc, ins[2], ins[3], panel, copy)
    p = msg.reshape(cols, W)
    wait(run([copy(ins[0].at[:, pl.ds(msg.shape[1], msg.shape[1])], msg), copy(ins[1], linv)]))
    ls = split(linv[...])
    for b in range(cols // WIDE):
        sl = slice(b * WIDE, (b + 1) * WIDE)
        at = iota2((W, WIDE), 1) + (rc[1] * cols + b * WIDE - W)
        x = three(ls, split(p[sl]), 1, 1)
        x = jnp.where(at < 0, 0.0, x) - jnp.where(at == iota2((W, WIDE), 0), 1.0, 0.0)
        v[0, :, sl], v[1, :, sl] = split(x)
    last = run([copy(v, outs[0])])
    wait(more)
    clear_top(rc, panel)
    for k in range(rows // STEP):
        sl = slice(k * STEP, (k + 1) * STEP)
        ids = rc[0] * rows + k * STEP + iota2((STEP, W), 0)
        x = three(split(panel[sl]), ls, 1, 1) - jnp.where(ids - W == iota2((STEP, W), 1), 1.0, 0.0)
        left[0, sl], left[1, sl] = split(x)
    wait(last + run([copy(left, outs[1])]))


def inner_kernel(rc, ins, outs, bufs, copy):
    v, y, out, mine = bufs
    piece = y.shape[1]
    first = run([copy(ins[0], v), copy(ins[1], y)])
    wait(run([copy(ins[2], mine)]))
    more = run([copy(mine, outs[0].at[k, pl.ds(0, piece)]) for k in range(NC)])
    wait(first)
    out[...] = three((v[0], v[1]), split(y[...].reshape(v.shape[2], W)), 1, 0)
    wait(more + run([copy(out, outs[0].at[k, pl.ds(piece, W)]) for k in range(NC)]))


def sides_kernel(rc, ins, outs, bufs, copy):
    yc, coup, wide = bufs
    cols = wide.shape[1]
    wait(run([copy(ins[0], yc), copy(ins[1], coup)]))
    cs = split(coup[...])
    flat = yc.reshape(cols, W)
    for b in range(cols // WIDE):
        sl = slice(b * WIDE, (b + 1) * WIDE)
        wide[:, sl] = three(cs, split(flat[sl]), 1, 1)
    wait(run([copy(wide, outs[0])]))


def last_kernel(rc, ins, outs, bufs, copy):
    a_ref, msg_ref, coup_ref, left_ref, wide_ref, v_ref = ins
    buf, s, coup, yr, left, wide, right = bufs
    rows, cols = buf.shape
    piece = yr.shape[1]
    n = cols // WIDE
    small = run([copy(msg_ref.at[:, pl.ds(piece, W)], s), copy(coup_ref, coup)])
    lefts = run([copy(msg_ref.at[:, pl.ds(0, piece)], yr)])
    for i, part in enumerate((0, 1, 0)):
        lefts += run([copy(left_ref.at[part], left.at[:, pl.ds(2 * i * W, W)])])
    mid = run([copy(v_ref, right), copy(wide_ref, wide)])
    cut = [pl.ds(k * WIDE, WIDE) for k in range(n)]
    copies = run([copy(a_ref.at[:, cut[k]], buf.at[:, cut[k]]) for k in range(n)])
    wait(small)
    cs = split(coup[...])
    middle = three(split(three(cs, split(jnp.sum(s[...], 0)), 1, 0)), cs, 1, 1)
    ms = split(0.5 * (middle + middle.T))
    wait(lefts)
    high, low = split(three(split(yr[...].reshape(rows, W)), cs, 1, 1))
    for i, part in enumerate((high, low, high)):
        left[:, (2 * i + 1) * W : (2 * i + 2) * W] = part
    wait(mid)
    ends = []
    for k in range(n):
        sl = slice(k * WIDE, (k + 1) * WIDE)
        vh, vl = right[0, :, sl], right[1, :, sl]
        wh, wl = split(wide[:, sl] - three(ms, (vh, vl), 1, 0))
        three_parts = jnp.concatenate([wh, vh, wh, vh, wl, vl], 0)
        copies[k].wait()
        buf[:, sl] -= bdot(left[...], three_parts, 1, 0)
        ends += run([copy(buf.at[:, cut[k]], outs[0].at[:, cut[k]])])
    wait(ends)


def on_device(matrix):
    rows, cols = matrix.shape
    piece = cols // NR
    half = rows // 2
    r = lax.axis_index("prow")
    c = lax.axis_index("pcol")
    axes = ("prow", "pcol")
    holds_top = (c == 0) | (c == 2) | (c == 4) | (c == 7)
    rc = jnp.stack([r, c, jnp.where(holds_top, 0, half)])
    big = 6 * rows * cols * W

    top, bot = matrix[:half, :W], matrix[half:, :W]
    to1 = lax.ppermute(bot, "pcol", [(0, 1)])
    to2 = lax.ppermute(top, "pcol", [(0, 2)])
    to6 = lax.ppermute(bot, "pcol", [(0, 6)])
    f_msg = call(
        second_kernel, "second", W, (rc, matrix), shape(NR, piece, W), [shape(W, cols), shape(cols, W)], 1 + NR
    )
    send = jnp.where(c == 0, top, jnp.where(c == 1, to1, jnp.where(c == 2, to2, to6)))
    f_msg, send = lax.optimization_barrier((f_msg, send))
    f_msg = lax.all_to_all(f_msg, "prow", 0, 0, tiled=True)
    got = lax.ppermute(send, "pcol", [(0, 7), (1, 3), (2, 4), (6, 5)])
    held = jnp.where((c == 0) | (c == 1) | (c == 2) | (c == 6), send, got)
    other = lax.ppermute(held, "pcol", [(i, i ^ 1) for i in range(NC)])
    owner = [(8 * ((g // NC) % 2) + g % NC) * NC + (g // NC) // 2 for g in range(NR * NC)]

    at = (c % (NC // 2)) * piece
    mine = jnp.where(
        (c < NC // 2) == holds_top,
        lax.dynamic_slice_in_dim(held, at, piece, 0),
        lax.dynamic_slice_in_dim(other, at, piece, 0),
    )
    panel_q = lax.ppermute(mine, axes, list(enumerate(owner)))
    half_bufs = [shape(rows, W)]
    small = call(gram_kernel, "gram", 6 * rows * W * W, (rc, held, other), shape(NR, 16, W), half_bufs + [shape(NR, 16, W)], 3)
    small, f_q = lax.optimization_barrier((small, f_msg[0]))
    small = lax.all_to_all(small, "prow", 0, 0, tiled=True)
    small = call(
        mix_kernel,
        "mix",
        NR * 16 * W,
        (rc, small),
        shape(NR, 16, W),
        [shape(NR, 16, W), shape(16, W)],
        1 + NR,
    )
    small, held, other = lax.optimization_barrier((small, held, other))
    small = lax.all_to_all(small, "prow", 0, 0, tiled=True)
    msg = call(
        first_kernel,
        "first_pass",
        big,
        (rc, matrix, held, other, panel_q),
        shape(NR, 2 * piece, W),
        [shape(rows, cols), shape(rows, W), shape(W, cols), shape(cols, W), shape(piece, W)],
        3 + rows // STEP + 2 * NR,
    )
    msg = lax.all_to_all(msg, "prow", 0, 0, tiled=True)
    linv = call(factor_kernel, "factor", 8e9, (rc, small), shape(W, W), [shape(NR, 8, W), shape(W, W)], 2)
    coup = call(
        coupling_kernel, "coupling", 8e9, (rc, small, linv), shape(W, W), [shape(NR, 8, W), shape(W, W), shape(W, W)], 3
    )
    sums, linv, coup = lax.optimization_barrier((msg, linv, coup))
    msg, y_q = call(
        piece_kernel,
        "piece_image",
        msg.size,
        (rc, sums, linv, f_q),
        [shape(NR, piece, W), shape(piece, W)],
        [shape(NR, piece, W), shape(W, W), shape(piece, W), shape(piece, W)],
        3 + NR + 1,
    )
    y_p = lax.ppermute(y_q, axes, [(b, a) for a, b in enumerate(owner)])
    msg, y_p = lax.optimization_barrier((msg, y_p))
    msg = lax.all_to_all(msg, "prow", 0, 0, tiled=True)
    vt, left = call(
        vectors_kernel,
        "vectors",
        6 * (rows + cols) * W * W,
        (rc, sums, linv, held, other),
        [shape(2, W, cols, dtype=BF16), shape(2, rows, W, dtype=BF16)],
        [
            shape(NR, piece, W),
            shape(W, W),
            shape(2, W, cols, dtype=BF16),
            shape(rows, W),
            shape(2, rows, W, dtype=BF16),
        ],
        6,
    )
    end = call(
        inner_kernel,
        "inner",
        6 * cols * W * W,
        (rc, vt, msg, y_p),
        shape(NC, piece + W, W),
        [shape(2, W, cols, dtype=BF16), shape(NR, piece, W), shape(W, W), shape(piece, W)],
        3 + 2 * NC,
    )
    end = lax.all_to_all(end, "pcol", 0, 0, tiled=True)
    wide = call(
        sides_kernel,
        "sides",
        6 * cols * W * W,
        (rc, msg, coup),
        shape(W, cols),
        [shape(NR, piece, W), shape(W, W), shape(W, cols)],
        3,
    )
    return call(
        last_kernel,
        "last_pass",
        2 * big,
        (rc, matrix, end, coup, left, wide, vt),
        shape(rows, cols),
        [
            shape(rows, cols),
            shape(NC, W, W),
            shape(W, W),
            shape(NC, piece, W),
            shape(rows, 6 * W, dtype=BF16),
            shape(W, cols),
            shape(2, W, cols, dtype=BF16),
        ],
        8 + 2 * (cols // WIDE),
    )


def solution(mesh):
    return jax.shard_map(
        on_device, mesh=mesh, in_specs=(P("prow", "pcol"),), out_specs=P("prow", "pcol"), check_vma=False
    )
```
